512 devices in a mesh: head: 8 (over z), resp: 64 (over x, y, core).
Axes of the slice: x: 4, y: 8, z: 8, core: 2. Of those that a mesh axis runs over, the one named last changes fastest.
Arguments:
- queries: bfloat16 [8192, 8192], P('resp', 'head'), may hold values from -48 to 48
- response_keys: bfloat16 [8192, 1024], P('resp', 'head'), may hold values from -6 to 6
- response_values: bfloat16 [8192, 1024], P('resp', 'head'), may hold values from -6 to 6
- cotangent: bfloat16 [8192, 8192], P('resp', 'head'), may hold values from -40 to 40
- prefix_keys: bfloat16 [2048, 1024], P(('head', 'resp')), may hold values from -10 to 10
- shared_prefix_values: bfloat16 [2048, 1024], P(('head', 'resp')), may hold values from -6 to 6
- lengths: int32 [64], P('resp'), may hold values from 32 to 128, as said below
- prefix_seen: int32 [64], P('resp'), may hold values from 1024 to 2048, as said below
Outputs:
- grad_queries: bfloat16 [8192, 8192], P('resp', 'head')
- response_key_gradient: bfloat16 [8192, 1024], P('resp', 'head')
- response_value_gradient: bfloat16 [8192, 1024], P('resp', 'head')
- prefix_key_gradient: float32 [2048, 1024], P(('head', 'resp'))
- prefix_value_gradient: float32 [2048, 1024], P(('head', 'resp'))
The draws below stay inside these ranges and needn't reach their ends.
Inputs may be any that keep to these rules, and one draw needn't show every extreme that they name: `lengths`: one response has all 128 tokens live and one has 32. `prefix_seen`: one response sees the whole prefix and one sees 2048 // 2 positions.
All inputs are finite; a program needn't handle non-finite values.
Results may differ from the reference program's by a relative error of at most 0.011.
Values may be sent and summed in bfloat16 or wider, within the bound.
No kernel may reach another device: no remote copies, remote signals or barrier semaphores. Data moves between devices by JAX's collectives and lax.ppermute only.
A program may use at most 64 MiB of HBM per device.

```python
import jax
import jax.numpy as jnp
from jax import lax

HEAD_WIDTH = 128
QUERY_GROUP = 8
RLEN = 128
KEY_VALUE_HEADS = 8
QUERY_HEADS = 64
RESP = 64
RESPONSE_TOKENS = 8192
PREFIX_LENGTH = 2048


def shared_keys(key):
    base_offset = jax.random.truncated_normal(key, -4.0, 4.0, (PREFIX_LENGTH, KEY_VALUE_HEADS * HEAD_WIDTH), jnp.float32)
    return base_offset


def draw_prefix_keys(key, part):
    base_offset = shared_keys(key)
    return base_offset.astype(jnp.bfloat16)


def draw_queries(key, part):
    own_key = jax.random.fold_in(key, 5)
    values = jax.random.truncated_normal(own_key, -4.0, 4.0, (RESPONSE_TOKENS, QUERY_HEADS * HEAD_WIDTH), jnp.float32)
    return values.astype(jnp.bfloat16)


def draw_lengths(key, part):
    key = jax.random.fold_in(key, 7)
    values = jax.random.randint(key, (RESP,), RLEN // 4, RLEN + 1)
    picks = jax.random.permutation(jax.random.fold_in(key, 1), RESP)
    return values.at[picks[0]].set(RLEN).at[picks[1]].set(RLEN // 4).astype(jnp.int32)


def draw_prefix_seen(key, part):
    key = jax.random.fold_in(key, 9)
    values = jax.random.randint(key, (RESP,), PREFIX_LENGTH // 2, PREFIX_LENGTH + 1)
    picks = jax.random.permutation(jax.random.fold_in(key, 1), RESP)
    return values.at[picks[0]].set(PREFIX_LENGTH).at[picks[1]].set(PREFIX_LENGTH // 2).astype(jnp.int32)


def block_scale(key, shape, pieces, least, largest):
    loudness = 1.0
    for dim, parts in pieces:
        steps = jax.random.uniform(jax.random.fold_in(jax.random.fold_in(key, 6), dim), (parts,), jnp.float32, least / len(pieces), largest / len(pieces))
        loudness = loudness * jnp.repeat(jnp.exp(steps), shape[dim] // parts).reshape((-1,) + (1,) * (len(shape) - 1 - dim))
    return loudness


def normal_values(stream_key, dims, spread, most, shards=(), kind=jnp.bfloat16):
    values = spread * jax.random.normal(stream_key, dims, jnp.float32)
    if shards:
        values = values * block_scale(stream_key, dims, shards, -0.22, 0.18)
    return jnp.clip(values, -most, most).astype(kind)


def setup_inputs(seed: int = 0) -> dict:
    key_list = jax.random.split(jax.random.key(seed), 9)
    return {
        "queries": draw_queries(jax.random.fold_in(key_list[8], 71), 0),
        "response_keys": normal_values(key_list[1], (RESPONSE_TOKENS, KEY_VALUE_HEADS * HEAD_WIDTH), 1.0, 6.0, ((0, 64), (1, 8))),
        "response_values": normal_values(key_list[2], (RESPONSE_TOKENS, KEY_VALUE_HEADS * HEAD_WIDTH), 1.0, 6.0, ((0, 64), (1, 8))),
        "cotangent": normal_values(key_list[3], (RESPONSE_TOKENS, QUERY_HEADS * HEAD_WIDTH), 8.0, 40.0, ((0, 64), (1, 8))),
        "prefix_keys": draw_prefix_keys(jax.random.fold_in(key_list[8], 71), 0),
        "shared_prefix_values": normal_values(key_list[5], (PREFIX_LENGTH, KEY_VALUE_HEADS * HEAD_WIDTH), 1.0, 6.0, ((0, 512),)),
        "lengths": draw_lengths(jax.random.fold_in(key_list[8], 71), 0),
        "prefix_seen": draw_prefix_seen(jax.random.fold_in(key_list[8], 71), 0),
    }


NEGATIVE = -1e30


def reference(queries, response_keys, response_values, cotangent, prefix_keys, shared_prefix_values, lengths, prefix_seen):
    factor = HEAD_WIDTH ** -0.5
    prefix_index = jnp.arange(PREFIX_LENGTH, dtype=jnp.int32)
    token_index = jnp.arange(RLEN, dtype=jnp.int32)
    row_token = jnp.tile(token_index, QUERY_GROUP)
    causal = row_token[:, None] >= token_index[None, :]

    def per_group(response, kv_head):
        row_off = (response * RLEN).astype(jnp.int32)
        col_off = (kv_head * QUERY_GROUP * HEAD_WIDTH).astype(jnp.int32)
        key_off = (kv_head * HEAD_WIDTH).astype(jnp.int32)
        zero = jnp.zeros((), jnp.int32)
        query_rows = lax.dynamic_slice(queries, (row_off, col_off), (RLEN, QUERY_GROUP * HEAD_WIDTH))
        grad_rows = lax.dynamic_slice(cotangent, (row_off, col_off), (RLEN, QUERY_GROUP * HEAD_WIDTH))
        live_rows = token_index < lengths[response]
        grad_rows = jnp.where(live_rows[:, None], grad_rows, jnp.zeros_like(grad_rows))
        query_stack = query_rows.reshape(RLEN, QUERY_GROUP, HEAD_WIDTH).transpose(1, 0, 2).reshape(QUERY_GROUP * RLEN, HEAD_WIDTH)
        grad_stack = grad_rows.reshape(RLEN, QUERY_GROUP, HEAD_WIDTH).transpose(1, 0, 2).reshape(QUERY_GROUP * RLEN, HEAD_WIDTH)
        pre_keys = lax.dynamic_slice(prefix_keys, (zero, key_off), (PREFIX_LENGTH, HEAD_WIDTH))
        pre_values = lax.dynamic_slice(shared_prefix_values, (zero, key_off), (PREFIX_LENGTH, HEAD_WIDTH))
        own_keys = lax.dynamic_slice(response_keys, (row_off, key_off), (RLEN, HEAD_WIDTH))
        own_values = lax.dynamic_slice(response_values, (row_off, key_off), (RLEN, HEAD_WIDTH))
        pre_scores = jnp.dot(query_stack, pre_keys.T, preferred_element_type=jnp.float32) * factor
        pre_scores = jnp.where((prefix_index < prefix_seen[response])[None, :], pre_scores, NEGATIVE)
        own_scores = jnp.dot(query_stack, own_keys.T, preferred_element_type=jnp.float32) * factor
        own_scores = jnp.where(causal, own_scores, NEGATIVE)
        row_peak = jnp.maximum(jnp.max(pre_scores, axis=1), jnp.max(own_scores, axis=1))
        row_total = jnp.sum(jnp.exp(pre_scores - row_peak[:, None]), axis=1) + jnp.sum(jnp.exp(own_scores - row_peak[:, None]), axis=1)
        log_total = row_peak + jnp.log(row_total)
        pre_probs = jnp.exp(pre_scores - log_total[:, None])
        own_probs = jnp.exp(own_scores - log_total[:, None])
        pre_gprobs = jnp.dot(grad_stack, pre_values.T, preferred_element_type=jnp.float32)
        own_gprobs = jnp.dot(grad_stack, own_values.T, preferred_element_type=jnp.float32)
        delta = jnp.sum(pre_probs * pre_gprobs, axis=1) + jnp.sum(own_probs * own_gprobs, axis=1)
        pre_gscores = pre_probs * (pre_gprobs - delta[:, None])
        own_gscores = own_probs * (own_gprobs - delta[:, None])
        pre_plow = pre_probs.astype(jnp.bfloat16)
        own_plow = own_probs.astype(jnp.bfloat16)
        pre_glow = pre_gscores.astype(jnp.bfloat16)
        own_glow = own_gscores.astype(jnp.bfloat16)
        query_gradient = (jnp.dot(pre_glow, pre_keys, preferred_element_type=jnp.float32) + jnp.dot(own_glow, own_keys, preferred_element_type=jnp.float32)) * factor
        query_gradient = query_gradient.astype(jnp.bfloat16).reshape(QUERY_GROUP, RLEN, HEAD_WIDTH).transpose(1, 0, 2).reshape(RLEN, QUERY_GROUP * HEAD_WIDTH)
        self_key_gradient = (jnp.dot(own_glow.T, query_stack, preferred_element_type=jnp.float32) * factor).astype(jnp.bfloat16)
        self_value_gradient = jnp.dot(own_plow.T, grad_stack, preferred_element_type=jnp.float32).astype(jnp.bfloat16)
        prefix_key_partial = jnp.dot(pre_glow.T, query_stack, preferred_element_type=jnp.float32) * factor
        prefix_value_partial = jnp.dot(pre_plow.T, grad_stack, preferred_element_type=jnp.float32)
        return query_gradient, self_key_gradient, self_value_gradient, prefix_key_partial, prefix_value_partial

    def per_response(running, response):
        def single_head(kv_head):
            return per_group(response, kv_head)

        query_gradient, self_key_gradient, self_value_gradient, prefix_key_partial, prefix_value_partial = lax.map(single_head, jnp.arange(KEY_VALUE_HEADS, dtype=jnp.int32))
        return (running[0] + prefix_key_partial, running[1] + prefix_value_partial), (query_gradient, self_key_gradient, self_value_gradient)

    initial_totals = (jnp.zeros((KEY_VALUE_HEADS, PREFIX_LENGTH, HEAD_WIDTH), jnp.float32), jnp.zeros((KEY_VALUE_HEADS, PREFIX_LENGTH, HEAD_WIDTH), jnp.float32))
    (key_totals, value_totals), (query_grads, self_key_gradients, self_value_gradients) = lax.scan(per_response, initial_totals, jnp.arange(RESP, dtype=jnp.int32))
    grad_queries = query_grads.transpose(0, 2, 1, 3).reshape(RESPONSE_TOKENS, QUERY_HEADS * HEAD_WIDTH)
    response_key_gradient = self_key_gradients.transpose(0, 2, 1, 3).reshape(RESPONSE_TOKENS, KEY_VALUE_HEADS * HEAD_WIDTH)
    response_value_gradient = self_value_gradients.transpose(0, 2, 1, 3).reshape(RESPONSE_TOKENS, KEY_VALUE_HEADS * HEAD_WIDTH)
    prefix_key_gradient = key_totals.transpose(1, 0, 2).reshape(PREFIX_LENGTH, KEY_VALUE_HEADS * HEAD_WIDTH)
    prefix_value_gradient = value_totals.transpose(1, 0, 2).reshape(PREFIX_LENGTH, KEY_VALUE_HEADS * HEAD_WIDTH)
    return grad_queries, response_key_gradient, response_value_gradient, prefix_key_gradient, prefix_value_gradient
```

```python
import functools
import math

import jax
import jax.numpy as jnp
from jax import lax
from jax.experimental import pallas as pl
from jax.experimental.pallas import tpu as pltpu
from jax.sharding import Mesh, PartitionSpec as P

NEGATIVE = -1e30
F32 = jnp.float32
BF16 = jnp.bfloat16
TILE = 8
HALF = 4
CORES = 2
VMEM = pl.BlockSpec(memory_space=pltpu.VMEM)
SMEM = pl.BlockSpec(memory_space=pltpu.SMEM)


def dot(a, b, dims):
    return lax.dot_general(a, b, (dims, ((), ())), preferred_element_type=F32)


NT = ((1,), (1,))
NN = ((1,), (0,))


def pack_kernel(keys_ref, values_ref, out_ref, both):
    heads = keys_ref.shape[1] // 128
    span = out_ref.shape[0] // heads
    both[0:HALF, :] = keys_ref[...].astype(F32)
    both[HALF:TILE, :] = values_ref[...].astype(F32)
    for head in range(heads):
        tile = both[:, head * 128 : (head + 1) * 128]
        tiles = jnp.broadcast_to(tile[None], (span // TILE, TILE, 128))
        out_ref[head * span : (head + 1) * span, :] = tiles.reshape(span, 128).astype(BF16)


def split_messages(block):
    count = block.shape[0] // (2 * TILE)
    pairs = block.astype(F32).reshape(count, 2, TILE, 128)
    first, second = pairs[:, 0], pairs[:, 1]
    top = lax.broadcasted_iota(jnp.int32, first.shape, 1) < HALF
    keys = jnp.where(top, first, pltpu.roll(second, HALF, 1))
    values = jnp.where(top, pltpu.roll(first, HALF, 1), second)
    return (
        keys.reshape(count * TILE, 128).astype(BF16),
        values.reshape(count * TILE, 128).astype(BF16),
    )


def join_messages(keys, values):
    count = keys.shape[0] // TILE
    keys = keys.reshape(count, TILE, 128)
    values = values.reshape(count, TILE, 128)
    top = lax.broadcasted_iota(jnp.int32, keys.shape, 1) < HALF
    first = jnp.where(top, keys, pltpu.roll(values, HALF, 1))
    second = jnp.where(top, pltpu.roll(keys, HALF, 1), values)
    pairs = jnp.stack([first, second], axis=1)
    return pairs.reshape(2 * count * TILE, 128).astype(BF16)


def fold(block, op):
    rows, lanes = block.shape
    return op(block.reshape(rows // TILE, TILE, lanes), axis=0)


def grad_kernel(
    length_ref,
    seen_ref,
    q_ref,
    g_ref,
    own_k_ref,
    own_v_ref,
    mine_ref,
    theirs_ref,
    dq_ref,
    dok_ref,
    dov_ref,
    dmine_ref,
    dtheirs_ref,
    k_s,
    v_s,
    kt_s,
    q_s,
    g_s,
    w_s,
    p_s,
    dk_s,
    dv_s,
    *,
    core_axis,
    chunk,
):
    tokens = own_k_ref.shape[0]
    group = q_ref.shape[1] // 128
    half = mine_ref.shape[0] // 2
    key_count = tokens + 2 * half
    factor = 128 ** (-0.5)
    scale = factor * math.log2(math.e)
    length = length_ref[0]
    seen = seen_ref[0]
    core = lax.axis_index(core_axis)

    live = lax.broadcasted_iota(jnp.int32, (tokens, 128), 0) < length
    for head in range(group):
        q_s[head * tokens : (head + 1) * tokens, :] = q_ref[:, head * 128 : (head + 1) * 128]
        grad = g_ref[:, head * 128 : (head + 1) * 128].astype(F32)
        g_s[head * tokens : (head + 1) * tokens, :] = jnp.where(live, grad, 0.0).astype(BF16)
    k_s[0:tokens, :] = own_k_ref[...]
    v_s[0:tokens, :] = own_v_ref[...]
    kt_s[:, 0:tokens] = own_k_ref[...].astype(F32).T.astype(BF16)
    step = 256
    for block, ref in enumerate((mine_ref, theirs_ref)):
        for at in range(0, half, step):
            keys, values = split_messages(ref[2 * at : 2 * (at + step), :])
            row = tokens + block * half + at
            k_s[row : row + step, :] = keys
            v_s[row : row + step, :] = values
            kt_s[:, row : row + step] = keys.astype(F32).T.astype(BF16)

    lanes = 2 * tokens
    starts = [(0, tokens)] + [(row, chunk) for row in range(tokens, key_count, chunk)]

    def pair_body(pair, first):
        rows = pl.ds(pl.multiple_of(pair * lanes, lanes), lanes)
        q2 = q_s[rows, :]
        g2 = g_s[rows, :]
        peak = jnp.full((TILE, lanes), NEGATIVE, F32)
        for row, size in starts:
            s = dot(k_s[row : row + size, :], q2, NT)
            index = lax.broadcasted_iota(jnp.int32, (size, lanes), 0)
            if row == 0:
                token = lax.broadcasted_iota(jnp.int32, (size, lanes), 1) % tokens
                keep = index <= token
            else:
                block = (row - tokens) // half
                local = index + (row - tokens - block * half)
                side = core if block == 0 else 1 - core
                keep = (local // HALF) * TILE + local % HALF + side * HALF < seen
            s = jnp.where(keep, s, NEGATIVE)
            w_s[row : row + size, :] = s
            peak = jnp.maximum(peak, fold(s, jnp.max))
        peak = jnp.max(peak, axis=0, keepdims=True)
        total = jnp.zeros((TILE, lanes), F32)
        weighted = jnp.zeros((TILE, lanes), F32)
        for row, size in starts:
            gp = dot(v_s[row : row + size, :], g2, NT)
            w = jnp.exp2((w_s[row : row + size, :] - peak) * scale)
            w_s[row : row + size, :] = w
            p_s[row : row + size, :] = gp
            total = total + fold(w, jnp.sum)
            weighted = weighted + fold(w * gp, jnp.sum)
        inverse = 1.0 / jnp.sum(total, axis=0, keepdims=True)
        delta = jnp.sum(weighted, axis=0, keepdims=True) * inverse
        dqt = jnp.zeros((128, lanes), F32)
        for row, size in starts:
            probs = w_s[row : row + size, :] * inverse
            grads = probs * (p_s[row : row + size, :] - delta)
            probs = probs.astype(BF16)
            grads = grads.astype(BF16)
            dqt = dqt + dot(kt_s[:, row : row + size], grads, NN)
            dk = dot(grads, q2, NN)
            dv = dot(probs, g2, NN)
            if first:
                dk_s[row : row + size, :] = dk
                dv_s[row : row + size, :] = dv
            else:
                dk_s[row : row + size, :] += dk
                dv_s[row : row + size, :] += dv
        dqt = dqt * factor
        for sub in range(2):
            block = dqt[:, sub * tokens : (sub + 1) * tokens].T.astype(BF16)
            dq_ref[:, pl.ds(pl.multiple_of((pair * 2 + sub) * 128, 128), 128)] = block

    pair_body(0, True)

    def loop_body(pair, carry):
        pair_body(pair, False)
        return carry

    lax.fori_loop(1, group // 2, loop_body, 0)

    dok_ref[...] = (dk_s[0:tokens, :] * factor).astype(BF16)
    dov_ref[...] = dv_s[0:tokens, :].astype(BF16)
    for block, ref in enumerate((dmine_ref, dtheirs_ref)):
        for at in range(0, half, step):
            row = tokens + block * half + at
            ref[2 * at : 2 * (at + step), :] = join_messages(
                dk_s[row : row + step, :] * factor, dv_s[row : row + step, :]
            )


def sum_kernel(in_ref, keys_ref, values_ref):
    heads = keys_ref.shape[1] // 128
    span = in_ref.shape[0] // heads
    for head in range(heads):
        part = in_ref[head * span : (head + 1) * span, :].astype(F32)
        total = jnp.sum(part.reshape(span // TILE, TILE, 128), axis=0)
        keys_ref[:, head * 128 : (head + 1) * 128] = total[0:HALF, :]
        values_ref[:, head * 128 : (head + 1) * 128] = total[HALF:TILE, :]


def swap_cores(block):
    return lax.ppermute(block, "core", [(0, 1), (1, 0)])


def per_device(queries, own_keys, own_values, cotangent, prefix_keys, prefix_values, lengths, seen):
    tokens = own_keys.shape[0]
    group = queries.shape[1] // 128
    wide = ("head", "x", "y")
    peers = math.prod(lax.axis_size(axis) for axis in wide)
    rows = peers * TILE
    half = peers * HALF
    key_count = tokens + 2 * half
    messages = pl.pallas_call(
        pack_kernel,
        out_shape=jax.ShapeDtypeStruct((rows, 128), BF16),
        in_specs=[VMEM] * 2,
        out_specs=VMEM,
        scratch_shapes=[pltpu.VMEM((TILE, prefix_keys.shape[1]), F32)],
    )(prefix_keys, prefix_values)
    mine = lax.all_to_all(messages, wide, 0, 0, tiled=True)
    theirs = swap_cores(mine)
    dq, dok, dov, dmine, dtheirs = pl.pallas_call(
        functools.partial(grad_kernel, core_axis="core", chunk=256),
        out_shape=(
            jax.ShapeDtypeStruct(queries.shape, BF16),
            jax.ShapeDtypeStruct(own_keys.shape, BF16),
            jax.ShapeDtypeStruct(own_values.shape, BF16),
            jax.ShapeDtypeStruct((rows, 128), BF16),
            jax.ShapeDtypeStruct((rows, 128), BF16),
        ),
        in_specs=[SMEM] * 2 + [VMEM] * 6,
        out_specs=(VMEM,) * 5,
        scratch_shapes=[
            pltpu.VMEM((key_count, 128), BF16),
            pltpu.VMEM((key_count, 128), BF16),
            pltpu.VMEM((128, key_count), BF16),
            pltpu.VMEM((group * tokens, 128), BF16),
            pltpu.VMEM((group * tokens, 128), BF16),
            pltpu.VMEM((key_count, 2 * tokens), F32),
            pltpu.VMEM((key_count, 2 * tokens), F32),
            pltpu.VMEM((key_count, 128), F32),
            pltpu.VMEM((key_count, 128), F32),
        ],
        compiler_params=pltpu.CompilerParams(vmem_limit_bytes=40 * 1024 * 1024),
    )(lengths, seen, queries, cotangent, own_keys, own_values, mine, theirs)
    summed = (dmine.astype(F32) + swap_cores(dtheirs).astype(F32)).astype(BF16)
    back = lax.all_to_all(summed, wide, 0, 0, tiled=True)
    dkeys, dvalues = pl.pallas_call(
        sum_kernel,
        out_shape=(jax.ShapeDtypeStruct(prefix_keys.shape, F32),) * 2,
        in_specs=[VMEM],
        out_specs=(VMEM,) * 2,
    )(back)
    return dq, dok, dov, dkeys, dvalues


def solution(mesh):
    heads, responses = mesh.devices.shape
    y_size = 8
    x_size = responses // (y_size * CORES)
    split = Mesh(
        mesh.devices.reshape(heads, x_size, y_size, CORES), ("head", "x", "y", "core")
    )
    resp = ("x", "y", "core")
    spread = ("head", "x", "y", "core")
    return jax.shard_map(
        per_device,
        mesh=split,
        in_specs=(
            P(resp, "head"),
            P(resp, "head"),
            P(resp, "head"),
            P(resp, "head"),
            P(spread, None),
            P(spread, None),
            P(resp),
            P(resp),
        ),
        out_specs=(
            P(resp, "head"),
            P(resp, "head"),
            P(resp, "head"),
            P(spread, None),
            P(spread, None),
        ),
        check_vma=False,
    )
```

```python
import functools
import math

import jax
import jax.numpy as jnp
from jax import lax
from jax.experimental import pallas as pl
from jax.experimental.pallas import tpu as pltpu
from jax.sharding import Mesh, PartitionSpec as P

NEGATIVE = -1e30
F32 = jnp.float32
BF16 = jnp.bfloat16
TILE = 8
HALF = 4
CORES = 2
VMEM = pl.BlockSpec(memory_space=pltpu.VMEM)


def dot(a, b, dims):
    return lax.dot_general(a, b, (dims, ((), ())), preferred_element_type=F32)


NT = ((1,), (1,))
NN = ((1,), (0,))


def pack_kernel(keys_ref, values_ref, out_ref, both):
    heads = keys_ref.shape[1] // 128
    span = out_ref.shape[0] // heads
    both[0:HALF, :] = keys_ref[...].astype(F32)
    both[HALF:TILE, :] = values_ref[...].astype(F32)
    for head in range(heads):
        tile = both[:, head * 128 : (head + 1) * 128]
        tiles = jnp.broadcast_to(tile[None], (span // TILE, TILE, 128))
        out_ref[head * span : (head + 1) * span, :] = tiles.reshape(span, 128).astype(BF16)


def split_messages(block):
    count = block.shape[0] // (2 * TILE)
    pairs = block.astype(F32).reshape(count, 2, TILE, 128)
    first, second = pairs[:, 0], pairs[:, 1]
    top = lax.broadcasted_iota(jnp.int32, first.shape, 1) < HALF
    keys = jnp.where(top, first, pltpu.roll(second, HALF, 1))
    values = jnp.where(top, pltpu.roll(first, HALF, 1), second)
    return (
        keys.reshape(count * TILE, 128).astype(BF16),
        values.reshape(count * TILE, 128).astype(BF16),
    )


def join_messages(keys, values):
    count = keys.shape[0] // TILE
    keys = keys.reshape(count, TILE, 128)
    values = values.reshape(count, TILE, 128)
    top = lax.broadcasted_iota(jnp.int32, keys.shape, 1) < HALF
    first = jnp.where(top, keys, pltpu.roll(values, HALF, 1))
    second = jnp.where(top, pltpu.roll(keys, HALF, 1), values)
    pairs = jnp.stack([first, second], axis=1)
    return pairs.reshape(2 * count * TILE, 128).astype(BF16)


def fold(block, op):
    rows, lanes = block.shape
    return op(block.reshape(rows // TILE, TILE, lanes), axis=0)


def stack_kernel(length_ref, q_ref, g_ref, q_out, g_out):
    tokens = q_ref.shape[0]
    live = lax.broadcasted_iota(jnp.int32, (tokens, 128), 0) < length_ref[...]
    for head in range(q_ref.shape[1] // 128):
        rows = slice(head * tokens, (head + 1) * tokens)
        q_out[rows, :] = q_ref[:, head * 128 : (head + 1) * 128]
        grad = g_ref[:, head * 128 : (head + 1) * 128].astype(F32)
        g_out[rows, :] = jnp.where(live, grad, 0.0).astype(BF16)


def grad_kernel(
    seen_ref,
    q_ref,
    g_ref,
    own_k_ref,
    own_v_ref,
    mine_ref,
    theirs_ref,
    dq_ref,
    dok_ref,
    dov_ref,
    dmine_ref,
    dtheirs_ref,
    k_s,
    v_s,
    kt_s,
    w_s,
    p_s,
    dk_s,
    dv_s,
    *,
    core_axis,
    chunk,
    span,
):
    tokens = own_k_ref.shape[0]
    group = q_ref.shape[0] // tokens
    half = mine_ref.shape[0] // 2
    key_count = tokens + 2 * half
    factor = 128 ** (-0.5)
    scale = factor * math.log2(math.e)
    core = lax.axis_index(core_axis)

    k_s[0:tokens, :] = own_k_ref[...]
    v_s[0:tokens, :] = own_v_ref[...]
    kt_s[:, 0:tokens] = own_k_ref[...].astype(F32).T.astype(BF16)
    step = 256
    for block, ref in enumerate((mine_ref, theirs_ref)):
        for at in range(0, half, step):
            keys, values = split_messages(ref[2 * at : 2 * (at + step), :])
            row = tokens + block * half + at
            k_s[row : row + step, :] = keys
            v_s[row : row + step, :] = values
            kt_s[:, row : row + step] = keys.astype(F32).T.astype(BF16)

    lanes = span * tokens
    starts = [(0, tokens)] + [(row, chunk) for row in range(tokens, key_count, chunk)]
    inner = lax.broadcasted_iota(jnp.int32, (TILE, lanes), 0)
    spread = (inner // HALF) * TILE + inner % HALF
    seen = jnp.broadcast_to(seen_ref[...], (TILE, lanes))
    room = (seen - spread - core * HALF, seen - spread - (1 - core) * HALF)

    def hide(s, row, size):
        if row == 0:
            token = lax.broadcasted_iota(jnp.int32, (size, lanes), 1) % tokens
            index = lax.broadcasted_iota(jnp.int32, (size, lanes), 0)
            return jnp.where(index <= token, s, NEGATIVE)
        block = (row - tokens) // half
        local = row - tokens - block * half
        if local + size <= half // 2:
            return s
        count = size // TILE
        parts = s.reshape(count, TILE, lanes)
        place = 2 * (local + TILE * lax.broadcasted_iota(jnp.int32, parts.shape, 0))
        return jnp.where(place < room[block][None], parts, NEGATIVE).reshape(size, lanes)

    pairs = group // span

    class Block:
        def __init__(self, pair):
            self.pair = pair
            rows = slice(pair * lanes, (pair + 1) * lanes)
            self.rows = rows
            self.w, self.p = w_s.at[pair % 2], p_s.at[pair % 2]
            self.q, self.g = q_ref[rows, :], g_ref[rows, :]
            self.peak = jnp.full((TILE, lanes), NEGATIVE, F32)
            self.total = jnp.zeros((TILE, lanes), F32)
            self.weighted = jnp.zeros((TILE, lanes), F32)
            self.dqt = jnp.zeros((128, lanes), F32)

        def score(self, row, size):
            s = hide(dot(k_s[row : row + size, :], self.q, NT), row, size)
            self.w[row : row + size, :] = s
            self.peak = jnp.maximum(self.peak, fold(s, jnp.max))

        def top(self):
            self.peak = jnp.max(self.peak, axis=0, keepdims=True)

        def weigh(self, row, size):
            gp = dot(v_s[row : row + size, :], self.g, NT)
            w = jnp.exp2((self.w[row : row + size, :] - self.peak) * scale)
            self.w[row : row + size, :] = w
            self.p[row : row + size, :] = gp
            self.total = self.total + fold(w, jnp.sum)
            self.weighted = self.weighted + fold(w * gp, jnp.sum)

        def norm(self):
            self.inverse = 1.0 / jnp.sum(self.total, axis=0, keepdims=True)
            self.delta = jnp.sum(self.weighted, axis=0, keepdims=True) * self.inverse

        def grad(self, row, size):
            probs = self.w[row : row + size, :] * self.inverse
            grads = probs * (self.p[row : row + size, :] - self.delta)
            probs = probs.astype(BF16)
            grads = grads.astype(BF16)
            self.dqt = self.dqt + dot(kt_s[:, row : row + size], grads, NN)
            dk = dot(grads, self.q, NN)
            dv = dot(probs, self.g, NN)
            if self.pair == 0:
                dk_s[row : row + size, :] = dk
                dv_s[row : row + size, :] = dv
            else:
                dk_s[row : row + size, :] += dk
                dv_s[row : row + size, :] += dv

        def finish(self):
            dqt = self.dqt * factor
            for sub in range(span):
                head = self.pair * span + sub
                block = dqt[:, sub * tokens : (sub + 1) * tokens].T.astype(BF16)
                dq_ref[:, head * 128 : (head + 1) * 128] = block

    done = None
    for pair in range(pairs + 1):
        work = Block(pair) if pair < pairs else None
        if work:
            for at in starts:
                work.score(*at)
            work.top()
        for at in starts:
            if work:
                work.weigh(*at)
            if done:
                done.grad(*at)
        if work:
            work.norm()
        if done:
            done.finish()
        done = work

    dok_ref[...] = (dk_s[0:tokens, :] * factor).astype(BF16)
    dov_ref[...] = dv_s[0:tokens, :].astype(BF16)
    for block, ref in enumerate((dmine_ref, dtheirs_ref)):
        for at in range(0, half, step):
            row = tokens + block * half + at
            ref[2 * at : 2 * (at + step), :] = join_messages(
                dk_s[row : row + step, :] * factor, dv_s[row : row + step, :]
            )


def megabytes(count):
    return pltpu.CompilerParams(vmem_limit_bytes=count * 1024 * 1024)


def stack_call(lengths, queries, cotangent):
    tokens, width = queries.shape
    return pl.pallas_call(
        stack_kernel,
        out_shape=(jax.ShapeDtypeStruct((tokens * (width // 128), 128), BF16),) * 2,
        in_specs=[VMEM] * 3,
        out_specs=(VMEM,) * 2,
        compiler_params=megabytes(4),
    )(lengths.reshape(1, 1), queries, cotangent)


def grad_call(seen, q, g, own_keys, own_values, mine, theirs, chunk=512, span=4):
    tokens = own_keys.shape[0]
    stacked = q.shape[0]
    key_count = tokens + mine.shape[0]
    return pl.pallas_call(
        functools.partial(grad_kernel, core_axis="core", chunk=chunk, span=span),
        out_shape=(
            jax.ShapeDtypeStruct((tokens, stacked // tokens * 128), BF16),
            jax.ShapeDtypeStruct(own_keys.shape, BF16),
            jax.ShapeDtypeStruct(own_values.shape, BF16),
            jax.ShapeDtypeStruct(mine.shape, BF16),
            jax.ShapeDtypeStruct(theirs.shape, BF16),
        ),
        in_specs=[VMEM] * 7,
        out_specs=(VMEM,) * 5,
        scratch_shapes=[
            pltpu.VMEM((key_count, 128), BF16),
            pltpu.VMEM((key_count, 128), BF16),
            pltpu.VMEM((128, key_count), BF16),
            pltpu.VMEM((2, key_count, span * tokens), F32),
            pltpu.VMEM((2, key_count, span * tokens), F32),
            pltpu.VMEM((key_count, 128), F32),
            pltpu.VMEM((key_count, 128), F32),
        ],
        compiler_params=megabytes(40),
    )(seen.reshape(1, 1), q, g, own_keys, own_values, mine, theirs)


def sum_kernel(in_ref, keys_ref, values_ref):
    heads = keys_ref.shape[1] // 128
    span = in_ref.shape[0] // heads
    for head in range(heads):
        part = in_ref[head * span : (head + 1) * span, :].astype(F32)
        total = jnp.sum(part.reshape(span // TILE, TILE, 128), axis=0)
        keys_ref[:, head * 128 : (head + 1) * 128] = total[0:HALF, :]
        values_ref[:, head * 128 : (head + 1) * 128] = total[HALF:TILE, :]


def swap_cores(block):
    return lax.ppermute(block, "core", [(0, 1), (1, 0)])


def per_device(queries, own_keys, own_values, cotangent, prefix_keys, prefix_values, lengths, seen):
    wide = ("head", "x", "y")
    peers = math.prod(lax.axis_size(axis) for axis in wide)
    rows = peers * TILE
    messages = pl.pallas_call(
        pack_kernel,
        out_shape=jax.ShapeDtypeStruct((rows, 128), BF16),
        in_specs=[VMEM] * 2,
        out_specs=VMEM,
        scratch_shapes=[pltpu.VMEM((TILE, prefix_keys.shape[1]), F32)],
    )(prefix_keys, prefix_values)
    mine = lax.all_to_all(messages, wide, 0, 0, tiled=True)
    q, g = stack_call(lengths, queries, cotangent)
    theirs = swap_cores(mine)
    dq, dok, dov, dmine, dtheirs = grad_call(
        seen, q, g, own_keys, own_values, mine, theirs
    )
    summed = (dmine.astype(F32) + swap_cores(dtheirs).astype(F32)).astype(BF16)
    back = lax.all_to_all(summed, wide, 0, 0, tiled=True)
    dkeys, dvalues = pl.pallas_call(
        sum_kernel,
        out_shape=(jax.ShapeDtypeStruct(prefix_keys.shape, F32),) * 2,
        in_specs=[VMEM],
        out_specs=(VMEM,) * 2,
        compiler_params=megabytes(4),
    )(back)
    return dq, dok, dov, dkeys, dvalues


def solution(mesh):
    heads, responses = mesh.devices.shape
    y_size = 8
    x_size = responses // (y_size * CORES)
    split = Mesh(
        mesh.devices.reshape(heads, x_size, y_size, CORES), ("head", "x", "y", "core")
    )
    resp = ("x", "y", "core")
    spread = ("head", "x", "y", "core")
    return jax.shard_map(
        per_device,
        mesh=split,
        in_specs=(
            P(resp, "head"),
            P(resp, "head"),
            P(resp, "head"),
            P(resp, "head"),
            P(spread, None),
            P(spread, None),
            P(resp),
            P(resp),
        ),
        out_specs=(
            P(resp, "head"),
            P(resp, "head"),
            P(resp, "head"),
            P(spread, None),
            P(spread, None),
        ),
        check_vma=False,
    )
```

```python
import functools
import math

import jax
import jax.numpy as jnp
from jax import lax
from jax.experimental import pallas as pl
from jax.experimental.pallas import tpu as pltpu
from jax.sharding import Mesh, PartitionSpec as P

NEGATIVE = -1e30
F32 = jnp.float32
BF16 = jnp.bfloat16
TILE = 8
HALF = 4
CORES = 2
VMEM = pl.BlockSpec(memory_space=pltpu.VMEM)


def dot(a, b, dims):
    return lax.dot_general(a, b, (dims, ((), ())), preferred_element_type=F32)


NT = ((1,), (1,))
NN = ((1,), (0,))


def pack_kernel(keys_ref, values_ref, out_ref, both):
    heads = keys_ref.shape[1] // 128
    span = out_ref.shape[0] // heads
    both[0:HALF, :] = keys_ref[...].astype(F32)
    both[HALF:TILE, :] = values_ref[...].astype(F32)
    for head in range(heads):
        tile = both[:, head * 128 : (head + 1) * 128]
        tiles = jnp.broadcast_to(tile[None], (span // TILE, TILE, 128))
        out_ref[head * span : (head + 1) * span, :] = tiles.reshape(span, 128).astype(BF16)


def split_messages(block):
    count = block.shape[0] // (2 * TILE)
    pairs = block.astype(F32).reshape(count, 2, TILE, 128)
    first, second = pairs[:, 0], pairs[:, 1]
    top = lax.broadcasted_iota(jnp.int32, first.shape, 1) < HALF
    keys = jnp.where(top, first, pltpu.roll(second, HALF, 1))
    values = jnp.where(top, pltpu.roll(first, HALF, 1), second)
    return (
        keys.reshape(count * TILE, 128).astype(BF16),
        values.reshape(count * TILE, 128).astype(BF16),
    )


def join_messages(keys, values):
    count = keys.shape[0] // TILE
    keys = keys.reshape(count, TILE, 128)
    values = values.reshape(count, TILE, 128)
    top = lax.broadcasted_iota(jnp.int32, keys.shape, 1) < HALF
    first = jnp.where(top, keys, pltpu.roll(values, HALF, 1))
    second = jnp.where(top, pltpu.roll(keys, HALF, 1), values)
    pairs = jnp.stack([first, second], axis=1)
    return pairs.reshape(2 * count * TILE, 128).astype(BF16)


def fold(block, op):
    rows, lanes = block.shape
    return op(block.reshape(rows // TILE, TILE, lanes), axis=0)


def stack_kernel(length_ref, q_ref, g_ref, q_out, g_out):
    tokens = q_ref.shape[0]
    live = lax.broadcasted_iota(jnp.int32, (tokens, 128), 0) < length_ref[...]
    for head in range(q_ref.shape[1] // 128):
        rows = slice(head * tokens, (head + 1) * tokens)
        q_out[rows, :] = q_ref[:, head * 128 : (head + 1) * 128]
        grad = g_ref[:, head * 128 : (head + 1) * 128].astype(F32)
        g_out[rows, :] = jnp.where(live, grad, 0.0).astype(BF16)


def grad_kernel(
    seen_ref,
    q_ref,
    g_ref,
    own_k_ref,
    own_v_ref,
    mine_ref,
    theirs_ref,
    dq_ref,
    dok_ref,
    dov_ref,
    dmine_ref,
    dtheirs_ref,
    k_s,
    v_s,
    kt_s,
    w_s,
    p_s,
    dk_s,
    dv_s,
    *,
    core_axis,
    chunk,
    span,
):
    tokens = own_k_ref.shape[0]
    group = q_ref.shape[0] // tokens
    half = mine_ref.shape[0] // 2
    key_count = tokens + 2 * half
    factor = 128 ** (-0.5)
    scale = factor * math.log2(math.e)
    core = lax.axis_index(core_axis)

    k_s[0:tokens, :] = own_k_ref[...]
    v_s[0:tokens, :] = own_v_ref[...]
    kt_s[:, 0:tokens] = own_k_ref[...].astype(F32).T.astype(BF16)
    step = 256
    for block, ref in enumerate((mine_ref, theirs_ref)):
        for at in range(0, half, step):
            keys, values = split_messages(ref[2 * at : 2 * (at + step), :])
            row = tokens + block * half + at
            k_s[row : row + step, :] = keys
            v_s[row : row + step, :] = values
            kt_s[:, row : row + step] = keys.astype(F32).T.astype(BF16)

    lanes = span * tokens
    starts = [(0, tokens)] + [(row, chunk) for row in range(tokens, key_count, chunk)]
    inner = lax.broadcasted_iota(jnp.int32, (TILE, lanes), 0)
    spread = (inner // HALF) * TILE + inner % HALF
    seen = jnp.broadcast_to(seen_ref[...], (TILE, lanes))
    room = (seen - spread - core * HALF, seen - spread - (1 - core) * HALF)

    def hide(s, row, size):
        if row == 0:
            token = lax.broadcasted_iota(jnp.int32, (size, lanes), 1) % tokens
            index = lax.broadcasted_iota(jnp.int32, (size, lanes), 0)
            return jnp.where(index <= token, s, NEGATIVE)
        block = (row - tokens) // half
        local = row - tokens - block * half
        if local + size <= half // 2:
            return s
        count = size // TILE
        parts = s.reshape(count, TILE, lanes)
        place = 2 * (local + TILE * lax.broadcasted_iota(jnp.int32, parts.shape, 0))
        return jnp.where(place < room[block][None], parts, NEGATIVE).reshape(size, lanes)

    pairs = group // span

    class Block:
        def __init__(self, pair):
            self.pair = pair
            rows = slice(pair * lanes, (pair + 1) * lanes)
            self.rows = rows
            self.w, self.p = w_s.at[pair % 2], p_s.at[pair % 2]
            self.q, self.g = q_ref[rows, :], g_ref[rows, :]
            self.peak = jnp.full((TILE, lanes), NEGATIVE, F32)
            self.total = jnp.zeros((TILE, lanes), F32)
            self.weighted = jnp.zeros((TILE, lanes), F32)
            self.dqt = jnp.zeros((128, lanes), F32)

        def score(self, row, size):
            s = hide(dot(k_s[row : row + size, :], self.q, NT), row, size)
            self.w[row : row + size, :] = s
            self.peak = jnp.maximum(self.peak, fold(s, jnp.max))

        def top(self):
            self.peak = jnp.max(self.peak, axis=0, keepdims=True)

        def weigh(self, row, size):
            gp = dot(v_s[row : row + size, :], self.g, NT)
            w = jnp.exp2((self.w[row : row + size, :] - self.peak) * scale)
            self.w[row : row + size, :] = w
            self.p[row : row + size, :] = gp
            self.total = self.total + fold(w, jnp.sum)
            self.weighted = self.weighted + fold(w * gp, jnp.sum)

        def norm(self):
            self.inverse = 1.0 / jnp.sum(self.total, axis=0, keepdims=True)
            self.delta = jnp.sum(self.weighted, axis=0, keepdims=True) * self.inverse

        def grad(self, row, size):
            probs = self.w[row : row + size, :] * self.inverse
            grads = probs * (self.p[row : row + size, :] - self.delta)
            probs = probs.astype(BF16)
            grads = grads.astype(BF16)
            self.dqt = self.dqt + dot(kt_s[:, row : row + size], grads, NN)
            dk = dot(grads, self.q, NN)
            dv = dot(probs, self.g, NN)
            if self.pair == 0:
                dk_s[row : row + size, :] = dk
                dv_s[row : row + size, :] = dv
            else:
                dk_s[row : row + size, :] += dk
                dv_s[row : row + size, :] += dv

        def finish(self):
            dqt = self.dqt * factor
            for sub in range(span):
                head = self.pair * span + sub
                block = dqt[:, sub * tokens : (sub + 1) * tokens].T.astype(BF16)
                dq_ref[:, head * 128 : (head + 1) * 128] = block

    done = None
    for pair in range(pairs + 1):
        work = Block(pair) if pair < pairs else None
        if work:
            for at in starts:
                work.score(*at)
            work.top()
        for at in starts:
            if work:
                work.weigh(*at)
            if done:
                done.grad(*at)
        if work:
            work.norm()
        if done:
            done.finish()
        done = work

    dok_ref[...] = (dk_s[0:tokens, :] * factor).astype(BF16)
    dov_ref[...] = dv_s[0:tokens, :].astype(BF16)
    for block, ref in enumerate((dmine_ref, dtheirs_ref)):
        for at in range(0, half, step):
            row = tokens + block * half + at
            ref[2 * at : 2 * (at + step), :] = join_messages(
                dk_s[row : row + step, :] * factor, dv_s[row : row + step, :]
            )


def megabytes(count):
    return pltpu.CompilerParams(vmem_limit_bytes=count * 1024 * 1024)


def stack_call(lengths, queries, cotangent):
    tokens, width = queries.shape
    return pl.pallas_call(
        stack_kernel,
        out_shape=(jax.ShapeDtypeStruct((tokens * (width // 128), 128), BF16),) * 2,
        in_specs=[VMEM] * 3,
        out_specs=(VMEM,) * 2,
        compiler_params=megabytes(4),
    )(lengths.reshape(1, 1), queries, cotangent)


def grad_call(seen, q, g, own_keys, own_values, mine, theirs, chunk=512, span=4):
    tokens = own_keys.shape[0]
    stacked = q.shape[0]
    key_count = tokens + mine.shape[0]
    return pl.pallas_call(
        functools.partial(grad_kernel, core_axis="core", chunk=chunk, span=span),
        out_shape=(
            jax.ShapeDtypeStruct((tokens, stacked // tokens * 128), BF16),
            jax.ShapeDtypeStruct(own_keys.shape, BF16),
            jax.ShapeDtypeStruct(own_values.shape, BF16),
            jax.ShapeDtypeStruct(mine.shape, BF16),
            jax.ShapeDtypeStruct(theirs.shape, BF16),
        ),
        in_specs=[VMEM] * 7,
        out_specs=(VMEM,) * 5,
        scratch_shapes=[
            pltpu.VMEM((key_count, 128), BF16),
            pltpu.VMEM((key_count, 128), BF16),
            pltpu.VMEM((128, key_count), BF16),
            pltpu.VMEM((2, key_count, span * tokens), F32),
            pltpu.VMEM((2, key_count, span * tokens), F32),
            pltpu.VMEM((key_count, 128), F32),
            pltpu.VMEM((key_count, 128), F32),
        ],
        compiler_params=megabytes(40),
    )(seen.reshape(1, 1), q, g, own_keys, own_values, mine, theirs)


def sum_kernel(in_ref, keys_ref, values_ref):
    heads = keys_ref.shape[1] // 128
    span = in_ref.shape[0] // heads
    for head in range(heads):
        part = in_ref[head * span : (head + 1) * span, :].astype(F32)
        total = jnp.sum(part.reshape(span // TILE, TILE, 128), axis=0)
        keys_ref[:, head * 128 : (head + 1) * 128] = total[0:HALF, :]
        values_ref[:, head * 128 : (head + 1) * 128] = total[HALF:TILE, :]


def swap_cores(block):
    return lax.ppermute(block, "core", [(0, 1), (1, 0)])


def per_device(queries, own_keys, own_values, cotangent, prefix_keys, prefix_values, lengths, seen):
    wide = ("head", "x", "y")
    peers = math.prod(lax.axis_size(axis) for axis in wide)
    rows = peers * TILE
    messages = pl.pallas_call(
        pack_kernel,
        out_shape=jax.ShapeDtypeStruct((rows, 128), BF16),
        in_specs=[VMEM] * 2,
        out_specs=VMEM,
        scratch_shapes=[pltpu.VMEM((TILE, prefix_keys.shape[1]), F32)],
    )(prefix_keys, prefix_values)
    mine = lax.all_to_all(messages, wide, 0, 0, tiled=True)
    q, g = stack_call(lengths, queries, cotangent)
    mine, q, g = lax.optimization_barrier((mine, q, g))
    theirs = swap_cores(mine)
    dq, dok, dov, dmine, dtheirs = grad_call(
        seen, q, g, own_keys, own_values, mine, theirs
    )
    summed = (dmine.astype(F32) + swap_cores(dtheirs).astype(F32)).astype(BF16)
    back = lax.all_to_all(summed, wide, 0, 0, tiled=True)
    dkeys, dvalues = pl.pallas_call(
        sum_kernel,
        out_shape=(jax.ShapeDtypeStruct(prefix_keys.shape, F32),) * 2,
        in_specs=[VMEM],
        out_specs=(VMEM,) * 2,
        compiler_params=megabytes(4),
    )(back)
    return dq, dok, dov, dkeys, dvalues


def solution(mesh):
    heads, responses = mesh.devices.shape
    y_size = 8
    x_size = responses // (y_size * CORES)
    split = Mesh(
        mesh.devices.reshape(heads, x_size, y_size, CORES), ("head", "x", "y", "core")
    )
    resp = ("x", "y", "core")
    spread = ("head", "x", "y", "core")
    return jax.shard_map(
        per_device,
        mesh=split,
        in_specs=(
            P(resp, "head"),
            P(resp, "head"),
            P(resp, "head"),
            P(resp, "head"),
            P(spread, None),
            P(spread, None),
            P(resp),
            P(resp),
        ),
        out_specs=(
            P(resp, "head"),
            P(resp, "head"),
            P(resp, "head"),
            P(spread, None),
            P(spread, None),
        ),
        check_vma=False,
    )
```

```python
import functools
import math

import jax
import jax.numpy as jnp
from jax import lax
from jax.experimental import pallas as pl
from jax.experimental.pallas import tpu as pltpu
from jax.sharding import Mesh, PartitionSpec as P

NEGATIVE = -1e30
F32 = jnp.float32
BF16 = jnp.bfloat16
TILE = 8
HALF = 4
CORES = 2
SPAN = 4
STEP = 256
VMEM = pl.BlockSpec(memory_space=pltpu.VMEM)


def dot(a, b, dims):
    return lax.dot_general(a, b, (dims, ((), ())), preferred_element_type=F32)


NT = ((1,), (1,))
NN = ((1,), (0,))


def pack_kernel(keys_ref, values_ref, out_ref, both):
    heads = keys_ref.shape[1] // 128
    span = out_ref.shape[0] // heads
    both[0:HALF, :] = keys_ref[...].astype(F32)
    both[HALF:TILE, :] = values_ref[...].astype(F32)
    for head in range(heads):
        tile = both[:, head * 128 : (head + 1) * 128]
        tiles = jnp.broadcast_to(tile[None], (span // TILE, TILE, 128))
        out_ref[head * span : (head + 1) * span, :] = tiles.reshape(span, 128).astype(BF16)


def split_messages(block):
    count = block.shape[0] // (2 * TILE)
    pairs = block.astype(F32).reshape(count, 2, TILE, 128)
    first, second = pairs[:, 0], pairs[:, 1]
    top = lax.broadcasted_iota(jnp.int32, first.shape, 1) < HALF
    keys = jnp.where(top, first, pltpu.roll(second, HALF, 1))
    values = jnp.where(top, pltpu.roll(first, HALF, 1), second)
    return (
        keys.reshape(count * TILE, 128).astype(BF16),
        values.reshape(count * TILE, 128).astype(BF16),
    )


def join_messages(keys, values):
    count = keys.shape[0] // TILE
    keys = keys.reshape(count, TILE, 128)
    values = values.reshape(count, TILE, 128)
    top = lax.broadcasted_iota(jnp.int32, keys.shape, 1) < HALF
    first = jnp.where(top, keys, pltpu.roll(values, HALF, 1))
    second = jnp.where(top, pltpu.roll(keys, HALF, 1), values)
    pairs = jnp.stack([first, second], axis=1)
    return pairs.reshape(2 * count * TILE, 128).astype(BF16)


def fold(block, op):
    rows, lanes = block.shape
    return op(block.reshape(rows // TILE, TILE, lanes), axis=0)


def stack_kernel(
    length_ref, seen_ref, q_ref, g_ref, k_ref, v_ref, q_out, g_out, seen_out, k_out, v_out
):
    tokens = q_ref.shape[0]
    k_out[...] = k_ref[...]
    v_out[...] = v_ref[...]
    seen_out[...] = jnp.broadcast_to(seen_ref[...], seen_out.shape)
    live = lax.broadcasted_iota(jnp.int32, (tokens, 128), 0) < length_ref[...]
    for head in range(q_ref.shape[1] // 128):
        rows = slice(head * tokens, (head + 1) * tokens)
        q_out[rows, :] = q_ref[:, head * 128 : (head + 1) * 128]
        grad = g_ref[:, head * 128 : (head + 1) * 128].astype(F32)
        g_out[rows, :] = jnp.where(live, grad, 0.0).astype(BF16)


def score_masks(seen, core, tokens, half, lanes):
    inner = lax.broadcasted_iota(jnp.int32, (TILE, lanes), 0)
    spread = (inner // HALF) * TILE + inner % HALF
    room = (seen - spread - core * HALF, seen - spread - (1 - core) * HALF)

    def hide(s, row, size):
        if row == 0:
            token = lax.broadcasted_iota(jnp.int32, (size, lanes), 1) % tokens
            index = lax.broadcasted_iota(jnp.int32, (size, lanes), 0)
            return jnp.where(index <= token, s, NEGATIVE)
        block = (row - tokens) // half
        local = row - tokens - block * half
        if local + size <= half // 2:
            return s
        count = size // TILE
        parts = s.reshape(count, TILE, lanes)
        place = 2 * (local + TILE * lax.broadcasted_iota(jnp.int32, parts.shape, 0))
        return jnp.where(place < room[block][None], parts, NEGATIVE).reshape(size, lanes)

    return hide


def early_kernel(
    seen_ref,
    q_ref,
    own_k_ref,
    own_v_ref,
    mine_ref,
    k_ref,
    v_ref,
    kt_ref,
    s_ref,
    peak_ref,
    *,
    core_axis,
    chunk,
    span,
):
    tokens = own_k_ref.shape[0]
    half = mine_ref.shape[0] // 2
    kept = tokens + half
    k_ref[0:tokens, :] = own_k_ref[...]
    v_ref[0:tokens, :] = own_v_ref[...]
    kt_ref[:, 0:tokens] = own_k_ref[...].astype(F32).T.astype(BF16)
    for at in range(0, half, STEP):
        keys, values = split_messages(mine_ref[2 * at : 2 * (at + STEP), :])
        row = tokens + at
        k_ref[row : row + STEP, :] = keys
        v_ref[row : row + STEP, :] = values
        kt_ref[:, row : row + STEP] = keys.astype(F32).T.astype(BF16)
    lanes = span * tokens
    hide = score_masks(seen_ref[...], lax.axis_index(core_axis), tokens, half, lanes)
    for pair in range(q_ref.shape[0] // lanes):
        rows = slice(pair * lanes, (pair + 1) * lanes)
        q = q_ref[rows, :]
        peak = jnp.full((TILE, lanes), NEGATIVE, F32)
        for row, size in [(0, tokens)] + [(row, chunk) for row in range(tokens, kept, chunk)]:
            s = hide(dot(k_ref[row : row + size, :], q, NT), row, size)
            s_ref[row : row + size, rows] = s
            peak = jnp.maximum(peak, fold(s, jnp.max))
        peak_ref[:, rows] = peak


def grad_kernel(
    seen_ref,
    q_ref,
    g_ref,
    v_ref,
    kt_ref,
    s_ref,
    peak_ref,
    theirs_ref,
    dqt_ref,
    dok_ref,
    dov_ref,
    dmine_ref,
    dtheirs_ref,
    k_s,
    v_s,
    kt_s,
    w_s,
    p_s,
    dk_s,
    dv_s,
    *,
    core_axis,
    chunk,
    span,
):
    half = theirs_ref.shape[0] // 2
    kept = v_ref.shape[0]
    tokens = kept - half
    group = q_ref.shape[0] // tokens
    key_count = tokens + 2 * half
    factor = 128 ** (-0.5)
    scale = factor * math.log2(math.e)
    step = STEP
    for at in range(0, half, step):
        keys, values = split_messages(theirs_ref[2 * at : 2 * (at + step), :])
        k_s[at : at + step, :] = keys
        v_s[at : at + step, :] = values
        kt_s[:, at : at + step] = keys.astype(F32).T.astype(BF16)

    lanes = span * tokens
    late = [(row, chunk) for row in range(kept, key_count, chunk)]
    starts = [(0, tokens)] + [(row, chunk) for row in range(tokens, kept, chunk)] + late
    hide = score_masks(seen_ref[...], lax.axis_index(core_axis), tokens, half, lanes)

    pairs = group // span

    class Block:
        def __init__(self, pair):
            self.pair = pair
            rows = slice(pair * lanes, (pair + 1) * lanes)
            self.rows = rows
            self.w, self.p = w_s.at[pair % 2], p_s.at[pair % 2]
            self.q, self.g = q_ref[rows, :], g_ref[rows, :]
            self.peak = peak_ref[:, rows]
            self.total = jnp.zeros((TILE, lanes), F32)
            self.weighted = jnp.zeros((TILE, lanes), F32)
            self.dqt = jnp.zeros((128, lanes), F32)

        def score(self, row, size):
            keys = k_s[row - kept : row - kept + size, :]
            s = hide(dot(keys, self.q, NT), row, size)
            self.w[row : row + size, :] = s
            self.peak = jnp.maximum(self.peak, fold(s, jnp.max))

        def top(self):
            self.peak = jnp.max(self.peak, axis=0, keepdims=True)

        def weigh(self, row, size):
            if row < kept:
                values = v_ref[row : row + size, :]
                s = s_ref[row : row + size, self.rows]
            else:
                values = v_s[row - kept : row - kept + size, :]
                s = self.w[row : row + size, :]
            gp = dot(values, self.g, NT)
            w = jnp.exp2((s - self.peak) * scale)
            self.w[row : row + size, :] = w
            self.p[row : row + size, :] = gp
            self.total = self.total + fold(w, jnp.sum)
            self.weighted = self.weighted + fold(w * gp, jnp.sum)

        def norm(self):
            self.inverse = 1.0 / jnp.sum(self.total, axis=0, keepdims=True)
            self.delta = jnp.sum(self.weighted, axis=0, keepdims=True) * self.inverse

        def grad(self, row, size):
            probs = self.w[row : row + size, :] * self.inverse
            grads = probs * (self.p[row : row + size, :] - self.delta)
            probs = probs.astype(BF16)
            grads = grads.astype(BF16)
            if row < kept:
                keys = kt_ref[:, row : row + size]
            else:
                keys = kt_s[:, row - kept : row - kept + size]
            self.dqt = self.dqt + dot(keys, grads, NN)
            dk = dot(grads, self.q, NN)
            dv = dot(probs, self.g, NN)
            if self.pair == 0:
                dk_s[row : row + size, :] = dk
                dv_s[row : row + size, :] = dv
            else:
                dk_s[row : row + size, :] += dk
                dv_s[row : row + size, :] += dv

        def finish(self):
            dqt_ref[:, self.rows] = self.dqt

    done = None
    for pair in range(pairs + 1):
        work = Block(pair) if pair < pairs else None
        if work:
            for at in late:
                work.score(*at)
            work.top()
        for at in starts:
            if work:
                work.weigh(*at)
            if done:
                done.grad(*at)
        if work:
            work.norm()
        if done:
            done.finish()
        done = work

    dok_ref[...] = dk_s[0:tokens, :]
    dov_ref[...] = dv_s[0:tokens, :]
    for block, ref in enumerate((dmine_ref, dtheirs_ref)):
        for at in range(0, half, step):
            row = tokens + block * half + at
            ref[2 * at : 2 * (at + step), :] = join_messages(
                dk_s[row : row + step, :] * factor, dv_s[row : row + step, :]
            )


def megabytes(count):
    return pltpu.CompilerParams(vmem_limit_bytes=count * 1024 * 1024)


def stack_call(lengths, seen, queries, cotangent, own_keys, own_values):
    tokens, width = queries.shape
    stacked = jax.ShapeDtypeStruct((tokens * (width // 128), 128), BF16)
    return pl.pallas_call(
        stack_kernel,
        out_shape=(
            stacked,
            stacked,
            jax.ShapeDtypeStruct((TILE, SPAN * tokens), jnp.int32),
            jax.ShapeDtypeStruct(own_keys.shape, BF16),
            jax.ShapeDtypeStruct(own_values.shape, BF16),
        ),
        in_specs=[VMEM] * 6,
        out_specs=(VMEM,) * 5,
        compiler_params=megabytes(4),
    )(lengths.reshape(1, 1), seen.reshape(1, 1), queries, cotangent, own_keys, own_values)


def early_call(seen, q, own_keys, own_values, mine, chunk=512, span=SPAN):
    kept = own_keys.shape[0] + mine.shape[0] // 2
    return pl.pallas_call(
        functools.partial(early_kernel, core_axis="core", chunk=chunk, span=span),
        out_shape=(
            jax.ShapeDtypeStruct((kept, 128), BF16),
            jax.ShapeDtypeStruct((kept, 128), BF16),
            jax.ShapeDtypeStruct((128, kept), BF16),
            jax.ShapeDtypeStruct((kept, q.shape[0]), F32),
            jax.ShapeDtypeStruct((TILE, q.shape[0]), F32),
        ),
        in_specs=[VMEM] * 5,
        out_specs=(VMEM,) * 5,
        compiler_params=megabytes(8),
    )(seen, q, own_keys, own_values, mine)


def grad_call(seen, q, g, values, keys_t, scores, peak, theirs, tokens, chunk=512, span=SPAN):
    stacked = q.shape[0]
    half = theirs.shape[0] // 2
    key_count = tokens + 2 * half
    return pl.pallas_call(
        functools.partial(grad_kernel, core_axis="core", chunk=chunk, span=span),
        out_shape=(
            jax.ShapeDtypeStruct((128, stacked), F32),
            jax.ShapeDtypeStruct((tokens, 128), F32),
            jax.ShapeDtypeStruct((tokens, 128), F32),
            jax.ShapeDtypeStruct(theirs.shape, BF16),
            jax.ShapeDtypeStruct(theirs.shape, BF16),
        ),
        in_specs=[VMEM] * 8,
        out_specs=(VMEM,) * 5,
        scratch_shapes=[
            pltpu.VMEM((half, 128), BF16),
            pltpu.VMEM((half, 128), BF16),
            pltpu.VMEM((128, half), BF16),
            pltpu.VMEM((2, key_count, span * tokens), F32),
            pltpu.VMEM((2, key_count, span * tokens), F32),
            pltpu.VMEM((key_count, 128), F32),
            pltpu.VMEM((key_count, 128), F32),
        ],
        compiler_params=megabytes(36),
    )(seen, q, g, values, keys_t, scores, peak, theirs)


def finish_kernel(dqt_ref, dk_ref, dv_ref, dq_ref, dok_ref, dov_ref):
    factor = 128 ** (-0.5)
    tokens = dk_ref.shape[0]
    for head in range(dq_ref.shape[1] // 128):
        block = dqt_ref[:, head * tokens : (head + 1) * tokens] * factor
        dq_ref[:, head * 128 : (head + 1) * 128] = block.T.astype(BF16)
    dok_ref[...] = (dk_ref[...] * factor).astype(BF16)
    dov_ref[...] = dv_ref[...].astype(BF16)


def finish_call(dqt, dk, dv, shape):
    return pl.pallas_call(
        finish_kernel,
        out_shape=(
            jax.ShapeDtypeStruct(shape, BF16),
            jax.ShapeDtypeStruct(dk.shape, BF16),
            jax.ShapeDtypeStruct(dv.shape, BF16),
        ),
        in_specs=[VMEM] * 3,
        out_specs=(VMEM,) * 3,
        compiler_params=megabytes(8),
    )(dqt, dk, dv)


def sum_kernel(in_ref, keys_ref, values_ref):
    heads = keys_ref.shape[1] // 128
    span = in_ref.shape[0] // heads
    for head in range(heads):
        part = in_ref[head * span : (head + 1) * span, :].astype(F32)
        total = jnp.sum(part.reshape(span // TILE, TILE, 128), axis=0)
        keys_ref[:, head * 128 : (head + 1) * 128] = total[0:HALF, :]
        values_ref[:, head * 128 : (head + 1) * 128] = total[HALF:TILE, :]


def swap_cores(block):
    return lax.ppermute(block, "core", [(0, 1), (1, 0)])


def per_device(queries, own_keys, own_values, cotangent, prefix_keys, prefix_values, lengths, seen):
    wide = ("head", "x", "y")
    peers = math.prod(lax.axis_size(axis) for axis in wide)
    rows = peers * TILE
    messages = pl.pallas_call(
        pack_kernel,
        out_shape=jax.ShapeDtypeStruct((rows, 128), BF16),
        in_specs=[VMEM] * 2,
        out_specs=VMEM,
        scratch_shapes=[pltpu.VMEM((TILE, prefix_keys.shape[1]), F32)],
    )(prefix_keys, prefix_values)
    mine = lax.all_to_all(messages, wide, 0, 0, tiled=True)
    staged = stack_call(lengths, seen, queries, cotangent, own_keys, own_values)
    mine, staged = lax.optimization_barrier((mine, staged))
    theirs = swap_cores(mine)
    q, g, seen, held_keys, held_values = staged
    early = early_call(seen, q, held_keys, held_values, mine)
    dqt, dk, dv, dmine, dtheirs = grad_call(seen, q, g, *early[1:], theirs, own_keys.shape[0])
    summed = (dmine.astype(F32) + swap_cores(dtheirs).astype(F32)).astype(BF16)
    summed, dqt, dk, dv = lax.optimization_barrier((summed, dqt, dk, dv))
    back = lax.all_to_all(summed, wide, 0, 0, tiled=True)
    dq, dok, dov = finish_call(dqt, dk, dv, queries.shape)
    dkeys, dvalues = pl.pallas_call(
        sum_kernel,
        out_shape=(jax.ShapeDtypeStruct(prefix_keys.shape, F32),) * 2,
        in_specs=[VMEM],
        out_specs=(VMEM,) * 2,
        compiler_params=megabytes(4),
    )(back)
    return dq, dok, dov, dkeys, dvalues


def solution(mesh):
    heads, responses = mesh.devices.shape
    y_size = 8
    x_size = responses // (y_size * CORES)
    split = Mesh(
        mesh.devices.reshape(heads, x_size, y_size, CORES), ("head", "x", "y", "core")
    )
    resp = ("x", "y", "core")
    spread = ("head", "x", "y", "core")
    return jax.shard_map(
        per_device,
        mesh=split,
        in_specs=(
            P(resp, "head"),
            P(resp, "head"),
            P(resp, "head"),
            P(resp, "head"),
            P(spread, None),
            P(spread, None),
            P(resp),
            P(resp),
        ),
        out_specs=(
            P(resp, "head"),
            P(resp, "head"),
            P(resp, "head"),
            P(spread, None),
            P(spread, None),
        ),
        check_vma=False,
    )
```

```python
import functools
import math

import jax
import jax.numpy as jnp
from jax import lax
from jax.experimental import pallas as pl
from jax.experimental.pallas import tpu as pltpu
from jax.sharding import Mesh, PartitionSpec as P

NEGATIVE = -1e30
F32 = jnp.float32
BF16 = jnp.bfloat16
TILE = 8
HALF = 4
CORES = 2
SPAN = 4
STEP = 256
VMEM = pl.BlockSpec(memory_space=pltpu.VMEM)


def dot(a, b, dims):
    return lax.dot_general(a, b, (dims, ((), ())), preferred_element_type=F32)


NT = ((1,), (1,))
NN = ((1,), (0,))


def pack_kernel(keys_ref, values_ref, out_ref, both):
    heads = keys_ref.shape[1] // 128
    span = out_ref.shape[0] // heads
    both[0:HALF, :] = keys_ref[...].astype(F32)
    both[HALF:TILE, :] = values_ref[...].astype(F32)
    for head in range(heads):
        tile = both[:, head * 128 : (head + 1) * 128]
        tiles = jnp.broadcast_to(tile[None], (span // TILE, TILE, 128))
        out_ref[head * span : (head + 1) * span, :] = tiles.reshape(span, 128).astype(BF16)


def split_messages(block):
    count = block.shape[0] // (2 * TILE)
    pairs = block.astype(F32).reshape(count, 2, TILE, 128)
    first, second = pairs[:, 0], pairs[:, 1]
    top = lax.broadcasted_iota(jnp.int32, first.shape, 1) < HALF
    keys = jnp.where(top, first, pltpu.roll(second, HALF, 1))
    values = jnp.where(top, pltpu.roll(first, HALF, 1), second)
    return (
        keys.reshape(count * TILE, 128).astype(BF16),
        values.reshape(count * TILE, 128).astype(BF16),
    )


def join_messages(keys, values):
    count = keys.shape[0] // TILE
    keys = keys.reshape(count, TILE, 128)
    values = values.reshape(count, TILE, 128)
    top = lax.broadcasted_iota(jnp.int32, keys.shape, 1) < HALF
    first = jnp.where(top, keys, pltpu.roll(values, HALF, 1))
    second = jnp.where(top, pltpu.roll(keys, HALF, 1), values)
    pairs = jnp.stack([first, second], axis=1)
    return pairs.reshape(2 * count * TILE, 128).astype(BF16)


def fold(block, op):
    rows, lanes = block.shape
    return op(block.reshape(rows // TILE, TILE, lanes), axis=0)


def stack_kernel(
    length_ref, seen_ref, q_ref, g_ref, k_ref, v_ref, q_out, g_out, seen_out, k_out, v_out
):
    tokens = q_ref.shape[0]
    k_out[...] = k_ref[...]
    v_out[...] = v_ref[...]
    seen_out[...] = jnp.broadcast_to(seen_ref[...], seen_out.shape)
    live = lax.broadcasted_iota(jnp.int32, (tokens, 128), 0) < length_ref[...]
    for head in range(q_ref.shape[1] // 128):
        rows = slice(head * tokens, (head + 1) * tokens)
        q_out[rows, :] = q_ref[:, head * 128 : (head + 1) * 128]
        grad = g_ref[:, head * 128 : (head + 1) * 128].astype(F32)
        g_out[rows, :] = jnp.where(live, grad, 0.0).astype(BF16)


def score_masks(seen, core, tokens, half, lanes):
    inner = lax.broadcasted_iota(jnp.int32, (TILE, lanes), 0)
    spread = (inner // HALF) * TILE + inner % HALF
    room = (seen - spread - core * HALF, seen - spread - (1 - core) * HALF)

    def hide(s, row, size):
        if row == 0:
            token = lax.broadcasted_iota(jnp.int32, (size, lanes), 1) % tokens
            index = lax.broadcasted_iota(jnp.int32, (size, lanes), 0)
            return jnp.where(index <= token, s, NEGATIVE)
        block = (row - tokens) // half
        local = row - tokens - block * half
        if local + size <= half // 2:
            return s
        count = size // TILE
        parts = s.reshape(count, TILE, lanes)
        place = 2 * (local + TILE * lax.broadcasted_iota(jnp.int32, parts.shape, 0))
        return jnp.where(place < room[block][None], parts, NEGATIVE).reshape(size, lanes)

    return hide


def early_kernel(
    seen_ref,
    q_ref,
    own_k_ref,
    own_v_ref,
    mine_ref,
    k_ref,
    v_ref,
    kt_ref,
    s_ref,
    peak_ref,
    *,
    core_axis,
    chunk,
    span,
):
    tokens = own_k_ref.shape[0]
    half = mine_ref.shape[0] // 2
    kept = tokens + half
    k_ref[0:tokens, :] = own_k_ref[...]
    v_ref[0:tokens, :] = own_v_ref[...]
    kt_ref[:, 0:tokens] = own_k_ref[...].astype(F32).T.astype(BF16)
    for at in range(0, half, STEP):
        keys, values = split_messages(mine_ref[2 * at : 2 * (at + STEP), :])
        row = tokens + at
        k_ref[row : row + STEP, :] = keys
        v_ref[row : row + STEP, :] = values
        kt_ref[:, row : row + STEP] = keys.astype(F32).T.astype(BF16)
    lanes = span * tokens
    hide = score_masks(seen_ref[...], lax.axis_index(core_axis), tokens, half, lanes)
    for pair in range(q_ref.shape[0] // lanes):
        rows = slice(pair * lanes, (pair + 1) * lanes)
        q = q_ref[rows, :]
        peak = jnp.full((TILE, lanes), NEGATIVE, F32)
        for row, size in [(0, tokens)] + [(row, chunk) for row in range(tokens, kept, chunk)]:
            s = hide(dot(k_ref[row : row + size, :], q, NT), row, size)
            s_ref[row : row + size, rows] = s
            peak = jnp.maximum(peak, fold(s, jnp.max))
        peak_ref[:, rows] = peak


def grad_kernel(
    seen_ref,
    q_ref,
    g_ref,
    v_ref,
    kt_ref,
    s_ref,
    peak_ref,
    theirs_ref,
    dqt_ref,
    dok_ref,
    dov_ref,
    dmine_ref,
    dtheirs_ref,
    k_s,
    v_s,
    kt_s,
    w_s,
    p_s,
    dk_s,
    dv_s,
    *,
    core_axis,
    chunk,
    span,
):
    half = theirs_ref.shape[0] // 2
    kept = v_ref.shape[0]
    tokens = kept - half
    group = q_ref.shape[0] // tokens
    key_count = tokens + 2 * half
    factor = 128 ** (-0.5)
    scale = factor * math.log2(math.e)
    step = STEP
    for at in range(0, half, step):
        keys, values = split_messages(theirs_ref[2 * at : 2 * (at + step), :])
        k_s[at : at + step, :] = keys
        v_s[at : at + step, :] = values
        kt_s[:, at : at + step] = keys.astype(F32).T.astype(BF16)

    lanes = span * tokens
    late = [(row, chunk) for row in range(kept, key_count, chunk)]
    starts = [(0, tokens)] + [(row, chunk) for row in range(tokens, kept, chunk)] + late
    hide = score_masks(seen_ref[...], lax.axis_index(core_axis), tokens, half, lanes)

    pairs = group // span

    class Block:
        def __init__(self, pair):
            self.pair = pair
            rows = slice(pair * lanes, (pair + 1) * lanes)
            self.rows = rows
            self.w, self.p = w_s.at[pair % 2], p_s.at[pair % 2]
            self.q, self.g = q_ref[rows, :], g_ref[rows, :]
            self.peak = peak_ref[:, rows]
            self.total = jnp.zeros((TILE, lanes), F32)
            self.weighted = jnp.zeros((TILE, lanes), F32)
            self.dqt = jnp.zeros((128, lanes), F32)

        def score(self, row, size):
            keys = k_s[row - kept : row - kept + size, :]
            s = hide(dot(keys, self.q, NT), row, size)
            self.w[row : row + size, :] = s
            self.peak = jnp.maximum(self.peak, fold(s, jnp.max))

        def top(self):
            self.peak = jnp.max(self.peak, axis=0, keepdims=True)

        def weigh(self, row, size):
            if row < kept:
                values = v_ref[row : row + size, :]
                s = s_ref[row : row + size, self.rows]
            else:
                values = v_s[row - kept : row - kept + size, :]
                s = self.w[row : row + size, :]
            gp = dot(values, self.g, NT)
            w = jnp.exp2((s - self.peak) * scale)
            self.w[row : row + size, :] = w
            self.p[row : row + size, :] = gp
            self.total = self.total + fold(w, jnp.sum)
            self.weighted = self.weighted + fold(w * gp, jnp.sum)

        def norm(self):
            self.inverse = 1.0 / jnp.sum(self.total, axis=0, keepdims=True)
            self.delta = jnp.sum(self.weighted, axis=0, keepdims=True) * self.inverse

        def grad(self, row, size):
            probs = self.w[row : row + size, :] * self.inverse
            grads = probs * (self.p[row : row + size, :] - self.delta)
            probs = probs.astype(BF16)
            grads = grads.astype(BF16)
            if row < kept:
                keys = kt_ref[:, row : row + size]
            else:
                keys = kt_s[:, row - kept : row - kept + size]
            self.dqt = self.dqt + dot(keys, grads, NN)
            dk = dot(grads, self.q, NN)
            dv = dot(probs, self.g, NN)
            if self.pair == 0:
                dk_s[row : row + size, :] = dk
                dv_s[row : row + size, :] = dv
            else:
                dk_s[row : row + size, :] += dk
                dv_s[row : row + size, :] += dv

        def finish(self):
            dqt_ref[:, self.rows] = self.dqt

    done = None
    for pair in range(pairs + 1):
        work = Block(pair) if pair < pairs else None
        if work:
            for at in late:
                work.score(*at)
            work.top()
        for at in starts:
            if work:
                work.weigh(*at)
            if done:
                done.grad(*at)
        if work:
            work.norm()
        if done:
            done.finish()
        done = work

    dok_ref[...] = dk_s[0:tokens, :]
    dov_ref[...] = dv_s[0:tokens, :]
    for block, ref in enumerate((dmine_ref, dtheirs_ref)):
        for at in range(0, half, step):
            row = tokens + block * half + at
            ref[2 * at : 2 * (at + step), :] = join_messages(
                dk_s[row : row + step, :] * factor, dv_s[row : row + step, :]
            )


def megabytes(count):
    return pltpu.CompilerParams(vmem_limit_bytes=count * 1024 * 1024)


def stack_call(lengths, seen, queries, cotangent, own_keys, own_values):
    tokens, width = queries.shape
    stacked = jax.ShapeDtypeStruct((tokens * (width // 128), 128), BF16)
    return pl.pallas_call(
        stack_kernel,
        out_shape=(
            stacked,
            stacked,
            jax.ShapeDtypeStruct((TILE, SPAN * tokens), jnp.int32),
            jax.ShapeDtypeStruct(own_keys.shape, BF16),
            jax.ShapeDtypeStruct(own_values.shape, BF16),
        ),
        in_specs=[VMEM] * 6,
        out_specs=(VMEM,) * 5,
        compiler_params=megabytes(4),
    )(lengths.reshape(1, 1), seen.reshape(1, 1), queries, cotangent, own_keys, own_values)


def early_call(seen, q, own_keys, own_values, mine, chunk=512, span=SPAN):
    kept = own_keys.shape[0] + mine.shape[0] // 2
    return pl.pallas_call(
        functools.partial(early_kernel, core_axis="core", chunk=chunk, span=span),
        out_shape=(
            jax.ShapeDtypeStruct((kept, 128), BF16),
            jax.ShapeDtypeStruct((kept, 128), BF16),
            jax.ShapeDtypeStruct((128, kept), BF16),
            jax.ShapeDtypeStruct((kept, q.shape[0]), F32),
            jax.ShapeDtypeStruct((TILE, q.shape[0]), F32),
        ),
        in_specs=[VMEM] * 5,
        out_specs=(VMEM,) * 5,
        compiler_params=megabytes(8),
    )(seen, q, own_keys, own_values, mine)


def grad_call(seen, q, g, values, keys_t, scores, peak, theirs, tokens, chunk=512, span=SPAN):
    stacked = q.shape[0]
    half = theirs.shape[0] // 2
    key_count = tokens + 2 * half
    return pl.pallas_call(
        functools.partial(grad_kernel, core_axis="core", chunk=chunk, span=span),
        out_shape=(
            jax.ShapeDtypeStruct((128, stacked), F32),
            jax.ShapeDtypeStruct((tokens, 128), F32),
            jax.ShapeDtypeStruct((tokens, 128), F32),
            jax.ShapeDtypeStruct(theirs.shape, BF16),
            jax.ShapeDtypeStruct(theirs.shape, BF16),
        ),
        in_specs=[VMEM] * 8,
        out_specs=(VMEM,) * 5,
        scratch_shapes=[
            pltpu.VMEM((half, 128), BF16),
            pltpu.VMEM((half, 128), BF16),
            pltpu.VMEM((128, half), BF16),
            pltpu.VMEM((2, key_count, span * tokens), F32),
            pltpu.VMEM((2, key_count, span * tokens), F32),
            pltpu.VMEM((key_count, 128), F32),
            pltpu.VMEM((key_count, 128), F32),
        ],
        compiler_params=megabytes(36),
    )(seen, q, g, values, keys_t, scores, peak, theirs)


def finish_kernel(dqt_ref, dk_ref, dv_ref, dq_ref, dok_ref, dov_ref):
    factor = 128 ** (-0.5)
    tokens = dk_ref.shape[0]
    for head in range(dq_ref.shape[1] // 128):
        block = dqt_ref[:, head * tokens : (head + 1) * tokens] * factor
        dq_ref[:, head * 128 : (head + 1) * 128] = block.T.astype(BF16)
    dok_ref[...] = (dk_ref[...] * factor).astype(BF16)
    dov_ref[...] = dv_ref[...].astype(BF16)


def finish_call(dqt, dk, dv, shape):
    return pl.pallas_call(
        finish_kernel,
        out_shape=(
            jax.ShapeDtypeStruct(shape, BF16),
            jax.ShapeDtypeStruct(dk.shape, BF16),
            jax.ShapeDtypeStruct(dv.shape, BF16),
        ),
        in_specs=[VMEM] * 3,
        out_specs=(VMEM,) * 3,
        compiler_params=megabytes(8),
    )(dqt, dk, dv)


def sum_kernel(in_ref, keys_ref, values_ref):
    heads = keys_ref.shape[1] // 128
    span = in_ref.shape[0] // heads
    for head in range(heads):
        part = in_ref[head * span : (head + 1) * span, :].astype(F32)
        total = jnp.sum(part.reshape(span // TILE, TILE, 128), axis=0)
        keys_ref[:, head * 128 : (head + 1) * 128] = total[0:HALF, :]
        values_ref[:, head * 128 : (head + 1) * 128] = total[HALF:TILE, :]


def swap_cores(block):
    return lax.ppermute(block, "core", [(0, 1), (1, 0)])


def per_device(queries, own_keys, own_values, cotangent, prefix_keys, prefix_values, lengths, seen):
    wide = ("head", "x", "y")
    peers = math.prod(lax.axis_size(axis) for axis in wide)
    rows = peers * TILE
    messages = pl.pallas_call(
        pack_kernel,
        out_shape=jax.ShapeDtypeStruct((rows, 128), BF16),
        in_specs=[VMEM] * 2,
        out_specs=VMEM,
        scratch_shapes=[pltpu.VMEM((TILE, prefix_keys.shape[1]), F32)],
    )(prefix_keys, prefix_values)
    mine = lax.all_to_all(messages, wide, 0, 0, tiled=True)
    staged = stack_call(lengths, seen, queries, cotangent, own_keys, own_values)
    mine, staged = lax.optimization_barrier((mine, staged))
    theirs = swap_cores(mine)
    q, g, seen, held_keys, held_values = staged
    early = early_call(seen, q, held_keys, held_values, mine)
    dqt, dk, dv, dmine, dtheirs = grad_call(seen, q, g, *early[1:], theirs, own_keys.shape[0])
    dq, dok, dov = finish_call(dqt, dk, dv, queries.shape)
    arrived, dok = lax.optimization_barrier((swap_cores(dtheirs), dok))
    summed = (dmine.astype(F32) + arrived.astype(F32)).astype(BF16)
    back = lax.all_to_all(summed, wide, 0, 0, tiled=True)
    dkeys, dvalues = pl.pallas_call(
        sum_kernel,
        out_shape=(jax.ShapeDtypeStruct(prefix_keys.shape, F32),) * 2,
        in_specs=[VMEM],
        out_specs=(VMEM,) * 2,
        compiler_params=megabytes(4),
    )(back)
    return dq, dok, dov, dkeys, dvalues


def solution(mesh):
    heads, responses = mesh.devices.shape
    y_size = 8
    x_size = responses // (y_size * CORES)
    split = Mesh(
        mesh.devices.reshape(heads, x_size, y_size, CORES), ("head", "x", "y", "core")
    )
    resp = ("x", "y", "core")
    spread = ("head", "x", "y", "core")
    return jax.shard_map(
        per_device,
        mesh=split,
        in_specs=(
            P(resp, "head"),
            P(resp, "head"),
            P(resp, "head"),
            P(resp, "head"),
            P(spread, None),
            P(spread, None),
            P(resp),
            P(resp),
        ),
        out_specs=(
            P(resp, "head"),
            P(resp, "head"),
            P(resp, "head"),
            P(spread, None),
            P(spread, None),
        ),
        check_vma=False,
    )
```

```python
import functools
import math

import jax
import jax.numpy as jnp
from jax import lax
from jax.experimental import pallas as pl
from jax.experimental.pallas import tpu as pltpu
from jax.sharding import Mesh, PartitionSpec as P

NEGATIVE = -1e30
F32 = jnp.float32
BF16 = jnp.bfloat16
TILE = 8
HALF = 4
CORES = 2
SPAN = 4
STEP = 256
VMEM = pl.BlockSpec(memory_space=pltpu.VMEM)


def dot(a, b, dims):
    return lax.dot_general(a, b, (dims, ((), ())), preferred_element_type=F32)


NT = ((1,), (1,))
NN = ((1,), (0,))


def pack_kernel(keys_ref, values_ref, out_ref, both):
    heads = keys_ref.shape[1] // 128
    span = out_ref.shape[0] // heads
    both[0:HALF, :] = keys_ref[...].astype(F32)
    both[HALF:TILE, :] = values_ref[...].astype(F32)
    for head in range(heads):
        tile = both[:, head * 128 : (head + 1) * 128]
        tiles = jnp.broadcast_to(tile[None], (span // TILE, TILE, 128))
        out_ref[head * span : (head + 1) * span, :] = tiles.reshape(span, 128).astype(BF16)


def split_messages(block):
    count = block.shape[0] // (2 * TILE)
    pairs = block.astype(F32).reshape(count, 2, TILE, 128)
    first, second = pairs[:, 0], pairs[:, 1]
    top = lax.broadcasted_iota(jnp.int32, first.shape, 1) < HALF
    keys = jnp.where(top, first, pltpu.roll(second, HALF, 1))
    values = jnp.where(top, pltpu.roll(first, HALF, 1), second)
    return (
        keys.reshape(count * TILE, 128).astype(BF16),
        values.reshape(count * TILE, 128).astype(BF16),
    )


def join_messages(keys, values):
    count = keys.shape[0] // TILE
    keys = keys.reshape(count, TILE, 128)
    values = values.reshape(count, TILE, 128)
    top = lax.broadcasted_iota(jnp.int32, keys.shape, 1) < HALF
    first = jnp.where(top, keys, pltpu.roll(values, HALF, 1))
    second = jnp.where(top, pltpu.roll(keys, HALF, 1), values)
    pairs = jnp.stack([first, second], axis=1)
    return pairs.reshape(2 * count * TILE, 128).astype(BF16)


def fold(block, op):
    rows, lanes = block.shape
    return op(block.reshape(rows // TILE, TILE, lanes), axis=0)


def stack_kernel(
    length_ref, seen_ref, q_ref, g_ref, k_ref, v_ref, q_out, g_out, seen_out, k_out, v_out
):
    tokens = q_ref.shape[0]
    k_out[...] = k_ref[...]
    v_out[...] = v_ref[...]
    seen_out[...] = jnp.broadcast_to(seen_ref[...], seen_out.shape)
    live = lax.broadcasted_iota(jnp.int32, (tokens, 128), 0) < length_ref[...]
    for head in range(q_ref.shape[1] // 128):
        rows = slice(head * tokens, (head + 1) * tokens)
        q_out[rows, :] = q_ref[:, head * 128 : (head + 1) * 128]
        grad = g_ref[:, head * 128 : (head + 1) * 128].astype(F32)
        g_out[rows, :] = jnp.where(live, grad, 0.0).astype(BF16)


def score_masks(seen, core, tokens, half, lanes):
    inner = lax.broadcasted_iota(jnp.int32, (TILE, lanes), 0)
    spread = (inner // HALF) * TILE + inner % HALF
    room = (seen - spread - core * HALF, seen - spread - (1 - core) * HALF)

    def hide(s, row, size):
        if row == 0:
            token = lax.broadcasted_iota(jnp.int32, (size, lanes), 1) % tokens
            index = lax.broadcasted_iota(jnp.int32, (size, lanes), 0)
            return jnp.where(index <= token, s, NEGATIVE)
        block = (row - tokens) // half
        local = row - tokens - block * half
        if local + size <= half // 2:
            return s
        count = size // TILE
        parts = s.reshape(count, TILE, lanes)
        place = 2 * (local + TILE * lax.broadcasted_iota(jnp.int32, parts.shape, 0))
        return jnp.where(place < room[block][None], parts, NEGATIVE).reshape(size, lanes)

    return hide


def early_kernel(
    seen_ref,
    q_ref,
    g_ref,
    own_k_ref,
    own_v_ref,
    mine_ref,
    k_ref,
    v_ref,
    kt_ref,
    s_ref,
    peak_ref,
    p_ref,
    *,
    core_axis,
    chunk,
    span,
):
    tokens = own_k_ref.shape[0]
    half = mine_ref.shape[0] // 2
    kept = tokens + half
    k_ref[0:tokens, :] = own_k_ref[...]
    v_ref[0:tokens, :] = own_v_ref[...]
    kt_ref[:, 0:tokens] = own_k_ref[...].astype(F32).T.astype(BF16)
    for at in range(0, half, STEP):
        keys, values = split_messages(mine_ref[2 * at : 2 * (at + STEP), :])
        row = tokens + at
        k_ref[row : row + STEP, :] = keys
        v_ref[row : row + STEP, :] = values
        kt_ref[:, row : row + STEP] = keys.astype(F32).T.astype(BF16)
    lanes = span * tokens
    hide = score_masks(seen_ref[...], lax.axis_index(core_axis), tokens, half, lanes)
    for pair in range(q_ref.shape[0] // lanes):
        rows = slice(pair * lanes, (pair + 1) * lanes)
        q = q_ref[rows, :]
        peak = jnp.full((TILE, lanes), NEGATIVE, F32)
        for row, size in [(0, tokens)] + [(row, chunk) for row in range(tokens, kept, chunk)]:
            s = hide(dot(k_ref[row : row + size, :], q, NT), row, size)
            s_ref[row : row + size, rows] = s
            peak = jnp.maximum(peak, fold(s, jnp.max))
        peak_ref[:, rows] = peak
        p_ref[:, rows] = dot(v_ref[0 : p_ref.shape[0], :], g_ref[rows, :], NT)


def grad_kernel(
    seen_ref,
    q_ref,
    g_ref,
    v_ref,
    kt_ref,
    s_ref,
    peak_ref,
    p_ref,
    theirs_ref,
    dqt_ref,
    dok_ref,
    dov_ref,
    dmine_ref,
    dtheirs_ref,
    k_s,
    v_s,
    kt_s,
    w_s,
    p_s,
    dk_s,
    dv_s,
    *,
    core_axis,
    chunk,
    span,
):
    half = theirs_ref.shape[0] // 2
    kept = v_ref.shape[0]
    tokens = kept - half
    group = q_ref.shape[0] // tokens
    key_count = tokens + 2 * half
    factor = 128 ** (-0.5)
    scale = factor * math.log2(math.e)
    step = STEP
    for at in range(0, half, step):
        keys, values = split_messages(theirs_ref[2 * at : 2 * (at + step), :])
        k_s[at : at + step, :] = keys
        v_s[at : at + step, :] = values
        kt_s[:, at : at + step] = keys.astype(F32).T.astype(BF16)

    lanes = span * tokens
    late = [(row, chunk) for row in range(kept, key_count, chunk)]
    starts = [(0, tokens)] + [(row, chunk) for row in range(tokens, kept, chunk)] + late
    hide = score_masks(seen_ref[...], lax.axis_index(core_axis), tokens, half, lanes)

    pairs = group // span

    class Block:
        def __init__(self, pair):
            self.pair = pair
            rows = slice(pair * lanes, (pair + 1) * lanes)
            self.rows = rows
            self.w, self.p = w_s.at[pair % 2], p_s.at[pair % 2]
            self.q, self.g = q_ref[rows, :], g_ref[rows, :]
            self.peak = peak_ref[:, rows]
            self.total = jnp.zeros((TILE, lanes), F32)
            self.weighted = jnp.zeros((TILE, lanes), F32)
            self.dqt = jnp.zeros((128, lanes), F32)

        def score(self, row, size):
            keys = k_s[row - kept : row - kept + size, :]
            s = hide(dot(keys, self.q, NT), row, size)
            self.w[row : row + size, :] = s
            self.peak = jnp.maximum(self.peak, fold(s, jnp.max))

        def top(self):
            self.peak = jnp.max(self.peak, axis=0, keepdims=True)

        def weigh(self, row, size):
            if row < kept:
                values = v_ref[row : row + size, :]
                s = s_ref[row : row + size, self.rows]
            else:
                values = v_s[row - kept : row - kept + size, :]
                s = self.w[row : row + size, :]
            ready = row < p_ref.shape[0]
            if ready:
                gp = p_ref[row : row + size, self.rows]
            else:
                gp = dot(values, self.g, NT)
                self.p[row : row + size, :] = gp
            w = jnp.exp2((s - self.peak) * scale)
            self.w[row : row + size, :] = w
            self.total = self.total + fold(w, jnp.sum)
            self.weighted = self.weighted + fold(w * gp, jnp.sum)

        def norm(self):
            self.inverse = 1.0 / jnp.sum(self.total, axis=0, keepdims=True)
            self.delta = jnp.sum(self.weighted, axis=0, keepdims=True) * self.inverse

        def grad(self, row, size):
            probs = self.w[row : row + size, :] * self.inverse
            if row < p_ref.shape[0]:
                gp = p_ref[row : row + size, self.rows]
            else:
                gp = self.p[row : row + size, :]
            grads = probs * (gp - self.delta)
            probs = probs.astype(BF16)
            grads = grads.astype(BF16)
            if row < kept:
                keys = kt_ref[:, row : row + size]
            else:
                keys = kt_s[:, row - kept : row - kept + size]
            self.dqt = self.dqt + dot(keys, grads, NN)
            dk = dot(grads, self.q, NN)
            dv = dot(probs, self.g, NN)
            if self.pair == 0:
                dk_s[row : row + size, :] = dk
                dv_s[row : row + size, :] = dv
            else:
                dk_s[row : row + size, :] += dk
                dv_s[row : row + size, :] += dv

        def finish(self):
            dqt_ref[:, self.rows] = self.dqt

    done = None
    for pair in range(pairs + 1):
        work = Block(pair) if pair < pairs else None
        if work:
            for at in late:
                work.score(*at)
            work.top()
        for at in starts:
            if work:
                work.weigh(*at)
            if done:
                done.grad(*at)
        if work:
            work.norm()
        if done:
            done.finish()
        done = work

    dok_ref[...] = dk_s[0:tokens, :]
    dov_ref[...] = dv_s[0:tokens, :]
    for block, ref in enumerate((dmine_ref, dtheirs_ref)):
        for at in range(0, half, step):
            row = tokens + block * half + at
            ref[2 * at : 2 * (at + step), :] = join_messages(
                dk_s[row : row + step, :] * factor, dv_s[row : row + step, :]
            )


def megabytes(count):
    return pltpu.CompilerParams(vmem_limit_bytes=count * 1024 * 1024)


def stack_call(lengths, seen, queries, cotangent, own_keys, own_values):
    tokens, width = queries.shape
    stacked = jax.ShapeDtypeStruct((tokens * (width // 128), 128), BF16)
    return pl.pallas_call(
        stack_kernel,
        out_shape=(
            stacked,
            stacked,
            jax.ShapeDtypeStruct((TILE, SPAN * tokens), jnp.int32),
            jax.ShapeDtypeStruct(own_keys.shape, BF16),
            jax.ShapeDtypeStruct(own_values.shape, BF16),
        ),
        in_specs=[VMEM] * 6,
        out_specs=(VMEM,) * 5,
        compiler_params=megabytes(4),
    )(lengths.reshape(1, 1), seen.reshape(1, 1), queries, cotangent, own_keys, own_values)


def early_call(seen, q, g, own_keys, own_values, mine, chunk=256, span=SPAN):
    kept = own_keys.shape[0] + mine.shape[0] // 2
    return pl.pallas_call(
        functools.partial(early_kernel, core_axis="core", chunk=chunk, span=span),
        out_shape=(
            jax.ShapeDtypeStruct((kept, 128), BF16),
            jax.ShapeDtypeStruct((kept, 128), BF16),
            jax.ShapeDtypeStruct((128, kept), BF16),
            jax.ShapeDtypeStruct((kept, q.shape[0]), F32),
            jax.ShapeDtypeStruct((TILE, q.shape[0]), F32),
            jax.ShapeDtypeStruct((own_keys.shape[0] + 512, q.shape[0]), F32),
        ),
        in_specs=[VMEM] * 6,
        out_specs=(VMEM,) * 6,
        compiler_params=megabytes(8),
    )(seen, q, g, own_keys, own_values, mine)


def grad_call(seen, q, g, values, keys_t, scores, peak, products, theirs, tokens, chunk=512, span=SPAN):
    stacked = q.shape[0]
    half = theirs.shape[0] // 2
    key_count = tokens + 2 * half
    return pl.pallas_call(
        functools.partial(grad_kernel, core_axis="core", chunk=chunk, span=span),
        out_shape=(
            jax.ShapeDtypeStruct((128, stacked), F32),
            jax.ShapeDtypeStruct((tokens, 128), F32),
            jax.ShapeDtypeStruct((tokens, 128), F32),
            jax.ShapeDtypeStruct(theirs.shape, BF16),
            jax.ShapeDtypeStruct(theirs.shape, BF16),
        ),
        in_specs=[VMEM] * 9,
        out_specs=(VMEM,) * 5,
        scratch_shapes=[
            pltpu.VMEM((half, 128), BF16),
            pltpu.VMEM((half, 128), BF16),
            pltpu.VMEM((128, half), BF16),
            pltpu.VMEM((2, key_count, span * tokens), F32),
            pltpu.VMEM((2, key_count, span * tokens), F32),
            pltpu.VMEM((key_count, 128), F32),
            pltpu.VMEM((key_count, 128), F32),
        ],
        compiler_params=megabytes(36),
    )(seen, q, g, values, keys_t, scores, peak, products, theirs)


def finish_kernel(dqt_ref, dk_ref, dv_ref, dq_ref, dok_ref, dov_ref):
    factor = 128 ** (-0.5)
    tokens = dk_ref.shape[0]
    for head in range(dq_ref.shape[1] // 128):
        block = dqt_ref[:, head * tokens : (head + 1) * tokens] * factor
        dq_ref[:, head * 128 : (head + 1) * 128] = block.T.astype(BF16)
    dok_ref[...] = (dk_ref[...] * factor).astype(BF16)
    dov_ref[...] = dv_ref[...].astype(BF16)


def finish_call(dqt, dk, dv, shape):
    return pl.pallas_call(
        finish_kernel,
        out_shape=(
            jax.ShapeDtypeStruct(shape, BF16),
            jax.ShapeDtypeStruct(dk.shape, BF16),
            jax.ShapeDtypeStruct(dv.shape, BF16),
        ),
        in_specs=[VMEM] * 3,
        out_specs=(VMEM,) * 3,
        compiler_params=megabytes(8),
    )(dqt, dk, dv)


def sum_kernel(in_ref, keys_ref, values_ref):
    heads = keys_ref.shape[1] // 128
    span = in_ref.shape[0] // heads
    for head in range(heads):
        part = in_ref[head * span : (head + 1) * span, :].astype(F32)
        total = jnp.sum(part.reshape(span // TILE, TILE, 128), axis=0)
        keys_ref[:, head * 128 : (head + 1) * 128] = total[0:HALF, :]
        values_ref[:, head * 128 : (head + 1) * 128] = total[HALF:TILE, :]


def swap_cores(block):
    return lax.ppermute(block, "core", [(0, 1), (1, 0)])


def per_device(queries, own_keys, own_values, cotangent, prefix_keys, prefix_values, lengths, seen):
    wide = ("head", "x", "y")
    peers = math.prod(lax.axis_size(axis) for axis in wide)
    rows = peers * TILE
    messages = pl.pallas_call(
        pack_kernel,
        out_shape=jax.ShapeDtypeStruct((rows, 128), BF16),
        in_specs=[VMEM] * 2,
        out_specs=VMEM,
        scratch_shapes=[pltpu.VMEM((TILE, prefix_keys.shape[1]), F32)],
    )(prefix_keys, prefix_values)
    mine = lax.all_to_all(messages, wide, 0, 0, tiled=True)
    staged = stack_call(lengths, seen, queries, cotangent, own_keys, own_values)
    mine, staged = lax.optimization_barrier((mine, staged))
    theirs = swap_cores(mine)
    q, g, seen, held_keys, held_values = staged
    early = early_call(seen, q, g, held_keys, held_values, mine)
    dqt, dk, dv, dmine, dtheirs = grad_call(seen, q, g, *early[1:], theirs, own_keys.shape[0])
    dq, dok, dov = finish_call(dqt, dk, dv, queries.shape)
    arrived, dok = lax.optimization_barrier((swap_cores(dtheirs), dok))
    summed = (dmine.astype(F32) + arrived.astype(F32)).astype(BF16)
    back = lax.all_to_all(summed, wide, 0, 0, tiled=True)
    dkeys, dvalues = pl.pallas_call(
        sum_kernel,
        out_shape=(jax.ShapeDtypeStruct(prefix_keys.shape, F32),) * 2,
        in_specs=[VMEM],
        out_specs=(VMEM,) * 2,
        compiler_params=megabytes(4),
    )(back)
    return dq, dok, dov, dkeys, dvalues


def solution(mesh):
    heads, responses = mesh.devices.shape
    y_size = 8
    x_size = responses // (y_size * CORES)
    split = Mesh(
        mesh.devices.reshape(heads, x_size, y_size, CORES), ("head", "x", "y", "core")
    )
    resp = ("x", "y", "core")
    spread = ("head", "x", "y", "core")
    return jax.shard_map(
        per_device,
        mesh=split,
        in_specs=(
            P(resp, "head"),
            P(resp, "head"),
            P(resp, "head"),
            P(resp, "head"),
            P(spread, None),
            P(spread, None),
            P(resp),
            P(resp),
        ),
        out_specs=(
            P(resp, "head"),
            P(resp, "head"),
            P(resp, "head"),
            P(spread, None),
            P(spread, None),
        ),
        check_vma=False,
    )
```
